128 devices in a mesh: tm: 16 (over y, z_hi, core), state: 8 (over z_lo, x).
Axes of the slice: x: 4, y: 4, z: 4 (z_hi: 2, z_lo: 2; z = z_hi * 2 + z_lo), core: 2. Of those that a mesh axis runs over, the one named last changes fastest.
Arguments:
- spikes: int32 [2304, 32768], P(None, 'tm'), may hold values from 0 to 3
- log_rate: bfloat16 [32768, 4096], P('tm', 'state'), may hold values from -0.03125 to 0.03125
- forward: bfloat16 [2304, 4096], P('tm', 'state'), may hold values from 0.019897461 to 1
- backward: float32 [2304, 4096], P('tm', 'state'), may hold values from 0.1 to 10
- transition: bfloat16 [4096, 4096], P(None, 'state'), may hold values from 0.049804688 to 1
- rate_total: float32 [4096], P('state'), may hold values from 0 to 3
- edge_weight: float32 [4096], P('state'), may hold values from 0.1 to 10
- block_mask: int32 [32, 32], replicated, may hold values 0 or 1
Outputs:
- transition_counts: float32 [4096, 4096], P('tm', 'state')
- pair_loglik: float32 [2304], P('tm')
The draws below stay inside these ranges and needn't reach their ends.
All inputs are finite; a program needn't handle non-finite values.
Results may differ from the reference program's by a relative error of at most 0.0005.
Values may be sent and summed in bfloat16 or wider, within the bound.
A program may use at most 128 MiB of HBM per device.

```python
import math
import jax
import jax.numpy as jnp

STATES = 4096
NEURONS = 32768
BLOCK = 128
TIME = 2304


def plant(result, stream_key, low, high):
    longest = result.shape.index(max(result.shape))
    spots = []
    for shift in (0, 1):
        where = [jax.random.randint(jax.random.fold_in(stream_key, axis), (), 0, length) for axis, length in enumerate(result.shape)]
        where[longest] = (where[longest] + shift) % result.shape[longest]
        spots.append(tuple(where))
    return result.at[spots[0]].set(low).at[spots[1]].set(high)


def levels(rng, dims, pieces, low, top_value):
    def one(position, shards_of):
        draws = jax.random.uniform(jax.random.fold_in(jax.random.fold_in(rng, 6), position), (shards_of,), jnp.float32, low / len(pieces), top_value / len(pieces))
        return jnp.repeat(jnp.exp(draws), dims[position] // shards_of).reshape((-1,) + (1,) * (len(dims) - position - 1))

    factor_of = one(*pieces[0])
    for cut in pieces[1:]:
        factor_of = factor_of * one(*cut)
    return factor_of


def bell_draw(key, dims, deviation, most, shards=(), kind=jnp.bfloat16):
    result = deviation * jax.random.normal(key, dims, jnp.float32)
    if shards:
        result = result * levels(key, dims, shards, -0.22, 0.18)
    return jnp.clip(result, -most, most).astype(kind)


def setup_inputs(seed: int = 0) -> dict:
    streams_of = jax.random.split(jax.random.key(seed), 9)
    return {
        "spikes": plant(jax.random.randint(streams_of[0], (TIME, NEURONS), 0, 4), jax.random.fold_in(streams_of[0], 1), 0, 3).astype(jnp.int32),
        "log_rate": bell_draw(streams_of[1], (NEURONS, STATES), NEURONS ** -0.5, 0.03125, ((0, 16), (1, 8))),
        "forward": jnp.clip(jnp.exp(math.log(1.0) - 3.9171631 * jax.random.uniform(streams_of[2], (TIME, STATES), jnp.float32) ** levels(streams_of[2], (TIME, STATES), ((0, 16), (1, 8)), -0.2, 0.2)), 0.019897461, 1.0).astype(jnp.bfloat16),
        "backward": jnp.clip(jnp.exp(math.log(10.0) - 4.6051702 * jax.random.uniform(streams_of[3], (TIME, STATES), jnp.float32) ** levels(streams_of[3], (TIME, STATES), ((0, 16), (1, 8)), -0.2, 0.2)), 0.1, 10.0),
        "transition": jnp.clip(jnp.exp(math.log(1.0) - 2.9996462 * jax.random.uniform(streams_of[4], (STATES, STATES), jnp.float32) ** levels(streams_of[4], (STATES, STATES), ((1, 8),), -0.2, 0.2)), 0.049804688, 1.0).astype(jnp.bfloat16),
        "rate_total": jnp.clip(3.0 * jax.random.uniform(streams_of[5], (STATES,), jnp.float32) ** levels(streams_of[5], (STATES,), ((0, 8),), -0.2, 0.2), 0.0, 3.0),
        "edge_weight": jnp.clip(jnp.exp(math.log(10.0) - 4.6051702 * jax.random.uniform(streams_of[6], (STATES,), jnp.float32) ** levels(streams_of[6], (STATES,), ((0, 8),), -0.2, 0.2)), 0.1, 10.0),
        "block_mask": plant((jax.random.randint(streams_of[7], (STATES // BLOCK, STATES // BLOCK), 0, 2) < 1).astype(jnp.int32), jax.random.fold_in(streams_of[7], 1), 0, 1),
    }


def reference(spikes, log_rate, forward, backward, transition, rate_total, edge_weight, block_mask):
    blocks = STATES // BLOCK
    allowed = jnp.maximum(block_mask, jnp.eye(blocks, dtype=jnp.int32))
    allowed = jnp.repeat(jnp.repeat(allowed, BLOCK, axis=0), BLOCK, axis=1)
    allowed_moves = transition * allowed.astype(transition.dtype)
    drive_sum = jnp.dot(spikes.astype(log_rate.dtype), log_rate, preferred_element_type=jnp.float32)
    right_term = jnp.exp(drive_sum - rate_total[None, :]) * backward
    ahead_bins = jnp.concatenate([right_term[1:], edge_weight[None, :]], axis=0)
    carried = jnp.dot(forward, allowed_moves, preferred_element_type=jnp.float32)
    totals = jnp.sum(carried * ahead_bins, axis=1)
    pair_loglik = jnp.log(totals)
    weights = (ahead_bins / totals[:, None]).astype(forward.dtype)
    pair_sums = jnp.dot(forward.T, weights, preferred_element_type=jnp.float32)
    count_scale = STATES * STATES / TIME
    transition_counts = allowed_moves.astype(jnp.float32) * pair_sums * count_scale
    return transition_counts, pair_loglik
```

```python
import functools
import jax
import jax.numpy as jnp
from jax import lax
from jax.experimental import pallas as pl
from jax.experimental.pallas import tpu as pltpu
from jax.sharding import PartitionSpec as P

MESH = pl.DeviceIdType.MESH
STATES = 4096
BLOCK = 128
F32, BF16, I16 = jnp.float32, jnp.bfloat16, jnp.int16
TOP = 32760.0
ROUND = 12582912.0
STEPS = ((2, 1), (1, 1), (3, 1), (0, 1), (2, 0), (1, 0), (3, 0), (0, 0))
YS = (2, 1, 3)


def encode(value):
    most = jnp.maximum(jnp.max(jnp.abs(value), axis=0, keepdims=True), 1e-30)
    coded = (value * (TOP / most) + ROUND) - ROUND
    return coded.astype(jnp.int32).astype(I16), jnp.broadcast_to(most * (1.0 / TOP), (8, value.shape[1]))


def decode(coded, scale):
    return coded.astype(jnp.int32).astype(F32) * scale[0:1, :]


def kernel(time_total, spikes, log_rate, forward, backward, transition, rate, edge, mask,
           counts, loglik,
           spk, lr, fw, bw, tr, am, rt, ew, out,
           tail, fg, fr, cs, cr, acc,
           p1s, p1r, p1sc, p1rc, q1s, q1r, q1sc, q1rc, q2s, q2r, q2sc, q2rc, p2s, p2r, p2sc, p2rc,
           car, tcol, tot, tsum, first, w,
           lsem, ssem, csem, tailsem, f1sem, f2sem, f3sem, p1sem, q1sem, q2sem, p2sem, totsem, firstsem, wsem, coresem):
    tm, st = lax.axis_index("tm"), lax.axis_index("state")
    y, zh, c = tm // 4, (tm // 2) % 2, tm % 2
    zl, x = st // 4, st % 4

    def at(dy=0, dz=0, dc=0):
        return (((y + dy) % 4) * 2 + (zh + dz) % 2) * 2 + (c + dc) % 2

    def sat(dx=0, dl=0):
        return ((zl + dl) % 2) * 4 + (x + dx) % 4

    rows = fw.shape[0]
    group = 2 * rows
    half = 256

    def local(src, dst, i):
        cp = pltpu.make_async_copy(src, dst, lsem.at[i])
        cp.start()
        return cp

    def spike_load(s):
        dy, dz = STEPS[s]
        row = pl.multiple_of((((y + dy) % 4) * 2 + (zh + dz) % 2) * group, group)
        return local(spikes.at[pl.ds(row, group), :], spk.at[s % spk.shape[0]], s % spk.shape[0])

    loads = {}
    load_fw = local(forward, fw, 4)
    load_lr = local(log_rate, lr, 5)
    for s in range(spk.shape[0]):
        loads[s] = spike_load(s)
    load_tr = local(transition, tr, 6)
    load_bw = local(backward, bw, 7)
    load_rt = local(rate, rt, 8)
    load_ew = local(edge, ew, 9)

    barrier = pltpu.get_barrier_semaphore()
    prev, nxt = (tm + 15) % 16, (tm + 1) % 16
    peers = [(at(dc=1), st)] + [(at(dy, dz, dc), st) for dy in range(4) for dz in range(2) for dc in range(2) if (dy, dz) != (0, 0)]
    peers += [(tm, sat(dx, dl)) for dx in range(4) for dl in range(2) if (dx, dl) != (0, 0)]
    for peer in peers:
        pl.semaphore_signal(barrier, inc=1, device_id=peer, device_id_type=MESH)
    pl.semaphore_wait(barrier, len(peers))

    sends = []

    def send(src, dst, rsem, device):
        i = len(sends)
        cp = pltpu.make_async_remote_copy(src, dst, ssem.at[i], rsem, device_id=device, device_id_type=MESH)
        cp.start()
        sends.append(cp)
        return cp

    def arrive(dst, rsem):
        pltpu.make_async_remote_copy(dst, dst, ssem.at[0], rsem, device_id=(tm, st), device_id_type=MESH).wait_recv()

    load_fw.wait()
    send(fw.at[pl.ds(rows - 16, 16), :], tail, tailsem.at[0], (nxt, st))
    load_lr.wait()

    def drive(s):
        loads[s].wait()
        part = jnp.dot(spk[s % spk.shape[0]].astype(F32).astype(BF16), lr[...], preferred_element_type=F32)
        parts = part.reshape(2, rows, 512)
        acc[s] = jnp.where(c == 0, parts[0], parts[1])
        cs[s] = jnp.where(c == 0, parts[1], parts[0])
        send(cs.at[s], cr.at[s], csem.at[s], (at(dc=1), st))
        if s + spk.shape[0] < 8:
            loads[s + spk.shape[0]] = spike_load(s + spk.shape[0])

    def pair_up(s):
        dy, dz = STEPS[s]
        arrive(cr.at[s], csem.at[s])
        if dy != 0:
            i = dz * 3 + dy - 1
            p1s[i], p1sc[i] = encode(acc[s, :, 0:half] + cr[s, :, 0:half])
            to = (at(dy), st)
            send(p1s.at[i], p1r.at[i], p1sem.at[0, i], to)
            send(p1sc.at[i], p1rc.at[i], p1sem.at[1, i], to)
        else:
            acc[s, :, 0:half] += cr[s, :, 0:half]
        if dz != 0:
            q1s[dy], q1sc[dy] = encode(acc[s, :, half:] + cr[s, :, half:])
            to = (at(0, 1), st)
            send(q1s.at[dy], q1r.at[dy], q1sem.at[0, dy], to)
            send(q1sc.at[dy], q1rc.at[dy], q1sem.at[1, dy], to)
        else:
            acc[s, :, half:] += cr[s, :, half:]

    def q_second(s):
        dy, _ = STEPS[s]
        arrive(q1r.at[dy], q1sem.at[0, dy])
        arrive(q1rc.at[dy], q1sem.at[1, dy])
        value = acc[s, :, half:] + decode(q1r[dy], q1rc[dy])
        if dy == 0:
            acc[s, :, half:] = value
        else:
            i = dy - 1
            q2s[i], q2sc[i] = encode(value)
            to = (at(dy), st)
            send(q2s.at[i], q2r.at[i], q2sem.at[0, i], to)
            send(q2sc.at[i], q2rc.at[i], q2sem.at[1, i], to)

    def p_sum(s):
        dz = STEPS[s][1]
        value = acc[s, :, 0:half]
        for dy in YS:
            i = dz * 3 + dy - 1
            arrive(p1r.at[i], p1sem.at[0, i])
            arrive(p1rc.at[i], p1sem.at[1, i])
            value = value + decode(p1r[i], p1rc[i])
        return value

    drive(0)
    arrive(tail, tailsem.at[0])
    turned = pltpu.roll(fw[...].astype(F32), 1, 0)
    above = jnp.broadcast_to(tail[...].astype(F32)[15:16, :], (rows, 512))
    at_top = lax.broadcasted_iota(jnp.int32, (rows, 512), 0) == 0
    fg[st] = jnp.where(at_top, above, turned).astype(BF16)
    send(fg.at[st], fg.at[st], f1sem.at[st], (tm, sat(0, 1)))
    for dx in (1, 3, 2):
        send(fg.at[st], fg.at[st], f1sem.at[st], (tm, sat(dx)))
    for s in range(1, 8):
        drive(s)
        pair_up(s - 1)
        if s == 2:
            other = sat(0, 1)
            arrive(fg.at[other], f1sem.at[other])
            for dx in (1, 3, 2):
                send(fg.at[other], fg.at[other], f1sem.at[other], (tm, sat(dx)))
        if s >= 6:
            q_second(s - 2)
    pair_up(7)
    q_second(6)
    value = p_sum(3)
    p2s[0], p2sc[0] = encode(value)
    to = (at(0, 1), st)
    send(p2s.at[0], p2r.at[0], p2sem.at[0], to)
    send(p2sc.at[0], p2rc.at[0], p2sem.at[1], to)
    q_second(7)

    load_tr.wait()

    @pl.loop(0, STATES // BLOCK)
    def _(ib):
        for cb in range(4):
            jb = st * 4 + cb
            keep = jnp.maximum(mask[ib, jb], (ib == jb).astype(jnp.int32)).astype(F32)
            at_rows = pl.ds(pl.multiple_of(ib * BLOCK, BLOCK), BLOCK)
            at_cols = pl.ds(cb * BLOCK, BLOCK)
            am[at_rows, at_cols] = (tr[at_rows, at_cols].astype(F32) * keep).astype(BF16)

    for dl in (0, 1):
        for dx in (1, 3, 2):
            who = sat(dx, dl)
            arrive(fg.at[who], f1sem.at[who])
    owner = x // 2
    quarter = x % 2
    mine = c == owner
    qcols = pl.ds(pl.multiple_of(x * 128, 128), 128)
    f2 = []
    for dy, dz in STEPS:
        i = len(sends)
        to_group = ((y + dy) % 4) * 2 + (zh + dz) % 2
        src = fg.at[to_group, :, qcols]
        dst = fr.at[quarter, tm]
        cp = pltpu.make_async_remote_copy(src, dst, ssem.at[i], f2sem.at[tm], device_id=(to_group * 2 + owner, st), device_id_type=MESH)
        sends.append(cp)
        if (dy, dz) != (0, 0):
            cp.start()
        else:
            own_cp = pltpu.make_async_copy(src, dst, f2sem.at[tm])
            pl.when(mine)(own_cp.start)
            pl.when(jnp.logical_not(mine))(cp.start)
            sends.pop()
            last_f2 = cp
            sends.append(None)
    car[...] = jnp.zeros_like(car)
    for b in range(8):
        car[...] += jnp.dot(fg[b], am[pl.ds(b * 512, 512), :], preferred_element_type=F32)

    load_bw.wait()
    load_rt.wait()
    load_ew.wait()
    value = p_sum(7)
    arrive(p2r.at[0], p2sem.at[0])
    arrive(p2rc.at[0], p2sem.at[1])
    p_drive = value + decode(p2r[0], p2rc[0])
    q_drive = acc[7, :, half:]
    for dy in YS:
        i = dy - 1
        arrive(q2r.at[i], q2sem.at[0, i])
        arrive(q2rc.at[i], q2sem.at[1, i])
        q_drive = q_drive + decode(q2r[i], q2rc[i])
    is_edge = jnp.logical_and(lax.broadcasted_iota(jnp.int32, (rows, half), 0) == 0, tm == 0)
    ahead = []
    total = jnp.zeros((rows, 1), F32)
    for h, drive_sum in enumerate((p_drive, q_drive)):
        cols = slice(h * half, (h + 1) * half)
        term = jnp.exp(drive_sum - rt[:, cols]) * bw[:, cols]
        term = jnp.where(is_edge, jnp.broadcast_to(ew[:, cols], (rows, half)), term)
        acc[0, :, cols] = term
        total = total + jnp.sum(term * car[:, cols], axis=1, keepdims=True)
    tcol[pl.ds(0, rows), :] = jnp.broadcast_to(total, (rows, 128))
    tcol[pl.ds(rows, 256 - rows), :] = jnp.ones((256 - rows, 128), F32)
    tot[st] = tcol[...].T[0:8, :]
    for dx, dl in ((2, 1), (2, 0), (1, 1), (3, 1), (1, 0), (3, 0), (0, 1)):
        send(tot.at[st], tot.at[st], totsem.at[st], (tm, sat(dx, dl)))

    @pl.when(mine)
    def _():
        pltpu.make_async_copy(fr.at[quarter, tm], fr.at[quarter, tm], f2sem.at[tm]).wait()
        for dy, dz in STEPS:
            for dc in range(2):
                if (dy, dz, dc) != (0, 0, 0):
                    arrive(fr.at[quarter, at(dy, dz, dc)], f2sem.at[at(dy, dz, dc)])
        for dx in (1, 3, 2):
            pltpu.make_async_remote_copy(fr.at[quarter], fr.at[quarter], f3sem.at[0, dx], f3sem.at[1, quarter],
                                         device_id=(tm, sat(dx)), device_id_type=MESH).start()

    for dx in range(4):
        for dl in range(2):
            if (dx, dl) != (0, 0):
                who = sat(dx, dl)
                arrive(tot.at[who], totsem.at[who])
    sums = tot[0]
    for b in range(1, 8):
        sums = sums + tot[b]
    tsum[...] = sums
    tcol[...] = jnp.broadcast_to(sums[0:1, :], (128, 256)).T
    norm = tcol[pl.ds(0, rows), :]
    for h in range(2):
        for q in range(2):
            cols = pl.ds(h * half + q * 128, 128)
            w[h, tm, :, pl.ds(q * 128, 128)] = (acc[0, :, cols] / norm).astype(BF16)

    def w_send(h, who, dy, dz, dc=0):
        send(w.at[h, who], w.at[h, who], (coresem if dc else wsem).at[h, who], (at(dy, dz, dc), st))

    def w_arrive(h, who, dc=0):
        arrive(w.at[h, who], (coresem if dc else wsem).at[h, who])

    w_send(0, tm, 0, 1)
    for dy in YS:
        w_send(1, tm, dy, 0)
    for dy in YS:
        w_send(0, tm, dy, 0)
    w_send(1, tm, 0, 1)
    w_send(0, tm, 0, 0, 1)
    w_send(1, tm, 0, 0, 1)
    send(tsum, first, firstsem.at[0], (prev, st))
    opp = at(0, 1)
    w_arrive(0, opp)
    for dy in YS:
        w_send(0, opp, dy, 0)
    w_send(0, opp, 0, 0, 1)
    for dy in (1, 3, 2):
        who = at(dy, 0)
        w_arrive(1, who)
        w_send(1, who, 0, 1)
        w_send(1, who, 0, 0, 1)
    for dy in (1, 3, 2):
        who = at(dy, 0)
        w_arrive(0, who)
        w_send(0, who, 0, 0, 1)
    w_arrive(1, opp)
    w_send(1, opp, 0, 0, 1)
    for dy in (1, 3, 2):
        for h in (0, 1):
            who = at(dy, 1)
            w_arrive(h, who)
            w_send(h, who, 0, 0, 1)

    arrive(first, firstsem.at[0])
    lanes = lax.broadcasted_iota(jnp.int32, (8, 256), 1)
    here = pltpu.roll(tsum[...], 255, 1)
    there = jnp.broadcast_to(first[...][:, 0:1], (8, 256))
    loglik[...] = jnp.log(jnp.where(lanes == rows - 1, there, here))

    for q in range(2):
        @pl.when(jnp.logical_not(jnp.logical_and(mine, quarter == q)))
        def _(q=q):
            pltpu.make_async_remote_copy(fr.at[q], fr.at[q], f3sem.at[0, 0], f3sem.at[1, q], device_id=(tm, st), device_id_type=MESH).wait_recv()
    for dy, dz in STEPS:
        for h in (0, 1):
            w_arrive(h, at(dy, dz, 1), 1)

    scale = STATES * STATES / time_total
    for h in range(2):
        right = w[h].reshape(16 * rows, half)
        for q in range(2):
            left = fr[q].reshape(16 * rows, 128)
            pair = lax.dot_general(left, right, (((0,), (0,)), ((), ())), preferred_element_type=F32)
            at_rows = pl.ds(pl.multiple_of(tm * 256 + q * 128, 128), 128)
            moves = am[at_rows, pl.ds(h * half, half)].astype(F32)
            out[pl.ds(q * 128, 128), pl.ds(h * half, half)] = moves * pair * scale
    store = local(out, counts, 10)

    for i, cp in enumerate(sends):
        if cp is not None:
            cp.wait_send()
    pl.when(jnp.logical_not(mine))(last_f2.wait_send)

    @pl.when(mine)
    def _():
        for dx in (1, 3, 2):
            pltpu.make_async_remote_copy(fr.at[quarter], fr.at[quarter], f3sem.at[0, dx], f3sem.at[1, quarter],
                                         device_id=(tm, sat(dx)), device_id_type=MESH).wait_send()
    store.wait()


def shards(spikes, log_rate, forward, backward, transition, rate_total, edge_weight, block_mask):
    rows = forward.shape[0]
    time_total = spikes.shape[0]
    neurons, width = log_rate.shape
    vm = pltpu.VMEM
    dma = pltpu.SemaphoreType.DMA
    scratch = [
        vm((3, 2 * rows, neurons), jnp.int32), vm((neurons, width), BF16), vm((rows, width), BF16), vm((rows, width), F32),
        vm((STATES, width), BF16), vm((STATES, width), BF16), vm((1, width), F32), vm((1, width), F32), vm((256, width), F32),
        vm((16, width), BF16), vm((8, rows, width), BF16), vm((2, 16, rows, 128), BF16),
        vm((8, rows, width), F32), vm((8, rows, width), F32), vm((8, rows, width), F32),
    ]
    for n in (6, 4, 3, 1):
        scratch += [vm((n, rows, 256), I16), vm((n, rows, 256), I16), vm((n, 8, 256), F32), vm((n, 8, 256), F32)]
    scratch += [
        vm((rows, width), F32), vm((256, 128), F32), vm((8, 8, 256), F32), vm((8, 256), F32), vm((8, 256), F32), vm((2, 16, rows, 256), BF16),
        dma((11,)), dma((120,)), dma((8,)), dma((1,)), dma((8,)), dma((16,)), dma((2, 4)), dma((2, 6)), dma((2, 4)), dma((2, 3)), dma((2,)),
        dma((8,)), dma((1,)), dma((2, 16)), dma((2, 16)),
    ]
    hbm = pl.BlockSpec(memory_space=pl.ANY)
    counts, loglik = pl.pallas_call(
        functools.partial(kernel, time_total),
        out_shape=(jax.ShapeDtypeStruct((256, width), F32), jax.ShapeDtypeStruct((8, 256), F32)),
        in_specs=[hbm] * 7 + [pl.BlockSpec(memory_space=pltpu.SMEM)],
        out_specs=(hbm, pl.BlockSpec(memory_space=pltpu.VMEM)),
        scratch_shapes=scratch,
        compiler_params=pltpu.CompilerParams(collective_id=0, has_side_effects=True, vmem_limit_bytes=56 * 2**20),
    )(spikes, log_rate, forward, backward, transition, rate_total.reshape(1, width), edge_weight.reshape(1, width), block_mask)
    return counts, loglik[0, :rows]


def solution(mesh):
    in_specs = (P(None, "tm"), P("tm", "state"), P("tm", "state"), P("tm", "state"), P(None, "state"), P("state"), P("state"), P())
    out_specs = (P("tm", "state"), P("tm"))
    return jax.shard_map(shards, mesh=mesh, in_specs=in_specs, out_specs=out_specs, check_vma=False)
```

```python
import functools
import jax
import jax.numpy as jnp
from jax import lax
from jax.experimental import pallas as pl
from jax.experimental.pallas import tpu as pltpu
from jax.sharding import PartitionSpec as P

MESH = pl.DeviceIdType.MESH
STATES = 4096
BLOCK = 128
F32, BF16, I16 = jnp.float32, jnp.bfloat16, jnp.int16
TOP = 32760.0
ROUND = 12582912.0
STEPS = ((2, 1), (1, 1), (3, 1), (0, 1), (2, 0), (1, 0), (3, 0), (0, 0))
YS = (2, 1, 3)
EARLY = 3
RELAY = 4


def encode(value):
    most = jnp.maximum(jnp.max(jnp.abs(value), axis=0, keepdims=True), 1e-30)
    coded = (value * (TOP / most) + ROUND) - ROUND
    return coded.astype(jnp.int32).astype(I16), jnp.broadcast_to(most * (1.0 / TOP), (8, value.shape[1]))


def decode(coded, scale):
    return coded.astype(jnp.int32).astype(F32) * scale[0:1, :]


def kernel(time_total, spikes, log_rate, forward, backward, transition, rate, edge, block_mask,
           counts, loglik,
           mask, lt, spk, lr, fw, bw, tr, am, rt, ew, out,
           tail, fg, fr, cs, cr, acc,
           p1s, p1r, p1sc, p1rc, q1s, q1r, q1sc, q1rc, q2s, q2r, q2sc, q2rc, p2s, p2r, p2sc, p2rc,
           car, tcol, tot, tsum, first, w,
           lsem, ssem, csem, tailsem, f1sem, f2sem, f3sem, p1sem, q1sem, q2sem, p2sem, totsem, firstsem, wsem, coresem):
    tm, st = lax.axis_index("tm"), lax.axis_index("state")
    y, zh, c = tm // 4, (tm // 2) % 2, tm % 2
    zl, x = st // 4, st % 4

    def at(dy=0, dz=0, dc=0):
        return (((y + dy) % 4) * 2 + (zh + dz) % 2) * 2 + (c + dc) % 2

    def sat(dx=0, dl=0):
        return ((zl + dl) % 2) * 4 + (x + dx) % 4

    rows = fw.shape[0]
    group = 2 * rows
    half = 256

    def local(src, dst, i):
        cp = pltpu.make_async_copy(src, dst, lsem.at[i])
        cp.start()
        return cp

    def spike_load(s):
        dy, dz = STEPS[s]
        row = pl.multiple_of((((y + dy) % 4) * 2 + (zh + dz) % 2) * group, group)
        return local(spikes.at[pl.ds(row, group), :], spk.at[s % spk.shape[0]], s % spk.shape[0])

    loads = {}
    load_fw = local(forward, fw, 8)
    load_lr = local(log_rate, lr, 9)
    for s in range(spk.shape[0]):
        loads[s] = spike_load(s)
    load_tr = local(transition, tr, 10)
    load_mask = local(block_mask, mask, 15)
    load_bw = local(backward, bw, 11)
    load_rt = local(rate, rt, 12)
    load_ew = local(edge, ew, 13)

    barrier = pltpu.get_barrier_semaphore()
    prev, nxt = (tm + 15) % 16, (tm + 1) % 16
    peers = [(at(dc=1), st)] + [(at(dy, dz, dc), st) for dy in range(4) for dz in range(2) for dc in range(2) if (dy != 0) != (dz != 0)]
    peers += [(tm, sat(dx, dl)) for dx in range(4) for dl in range(2) if (dx, dl) != (0, 0)]
    for peer in peers:
        pl.semaphore_signal(barrier, inc=1, device_id=peer, device_id_type=MESH)

    sends = []

    def send(src, dst, rsem, device):
        i = len(sends)
        cp = pltpu.make_async_remote_copy(src, dst, ssem.at[i], rsem, device_id=device, device_id_type=MESH)
        cp.start()
        sends.append(cp)
        return cp

    def arrive(dst, rsem):
        pltpu.make_async_remote_copy(dst, dst, ssem.at[0], rsem, device_id=(tm, st), device_id_type=MESH).wait_recv()


    def drive(s):
        loads[s].wait()
        part = jnp.dot(spk[s % spk.shape[0]].astype(F32).astype(BF16), lr[...], preferred_element_type=F32)
        parts = part.reshape(2, rows, 512)
        acc[s] = jnp.where(c == 0, parts[0], parts[1])
        cs[s] = jnp.where(c == 0, parts[1], parts[0])
        if s + spk.shape[0] < 8:
            loads[s + spk.shape[0]] = spike_load(s + spk.shape[0])

    def swap(s):
        send(cs.at[s], cr.at[s], csem.at[s], (at(dc=1), st))

    def pair_up(s):
        dy, dz = STEPS[s]
        arrive(cr.at[s], csem.at[s])
        if dy != 0:
            i = dz * 3 + dy - 1
            p1s[i], p1sc[i] = encode(acc[s, :, 0:half] + cr[s, :, 0:half])
            to = (at(dy), st)
            send(p1s.at[i], p1r.at[i], p1sem.at[0, i], to)
            send(p1sc.at[i], p1rc.at[i], p1sem.at[1, i], to)
        else:
            acc[s, :, 0:half] += cr[s, :, 0:half]
        if dz != 0:
            q1s[dy], q1sc[dy] = encode(acc[s, :, half:] + cr[s, :, half:])
            to = (at(0, 1), st)
            send(q1s.at[dy], q1r.at[dy], q1sem.at[0, dy], to)
            send(q1sc.at[dy], q1rc.at[dy], q1sem.at[1, dy], to)
        else:
            acc[s, :, half:] += cr[s, :, half:]

    def q_second(s):
        dy, _ = STEPS[s]
        arrive(q1r.at[dy], q1sem.at[0, dy])
        arrive(q1rc.at[dy], q1sem.at[1, dy])
        value = acc[s, :, half:] + decode(q1r[dy], q1rc[dy])
        if dy == 0:
            acc[s, :, half:] = value
        else:
            i = dy - 1
            q2s[i], q2sc[i] = encode(value)
            to = (at(dy), st)
            send(q2s.at[i], q2r.at[i], q2sem.at[0, i], to)
            send(q2sc.at[i], q2rc.at[i], q2sem.at[1, i], to)

    def p_sum(s):
        dz = STEPS[s][1]
        value = acc[s, :, 0:half]
        for dy in YS:
            i = dz * 3 + dy - 1
            arrive(p1r.at[i], p1sem.at[0, i])
            arrive(p1rc.at[i], p1sem.at[1, i])
            value = value + decode(p1r[i], p1rc[i])
        return value

    load_lr.wait()
    for s in range(EARLY):
        drive(s)
    load_fw.wait()
    fg[st] = fw[...]
    pl.semaphore_wait(barrier, len(peers))
    swap(0)
    send(fg.at[st], fg.at[st], f1sem.at[st], (tm, sat(0, 1)))
    for dx in (1, 3, 2):
        send(fg.at[st], fg.at[st], f1sem.at[st], (tm, sat(dx)))
    for s in range(1, EARLY):
        swap(s)
    other = sat(0, 1)
    for s in range(8):
        pair_up(s)
        if s + EARLY < 8:
            drive(s + EARLY)
            swap(s + EARLY)
        if s == RELAY:
            arrive(fg.at[other], f1sem.at[other])
            for dx in (1, 3, 2):
                send(fg.at[other], fg.at[other], f1sem.at[other], (tm, sat(dx)))
        if s >= 6:
            q_second(s - 2)
    q_second(6)
    value = p_sum(3)
    p2s[0], p2sc[0] = encode(value)
    to = (at(0, 1), st)
    send(p2s.at[0], p2r.at[0], p2sem.at[0], to)
    send(p2sc.at[0], p2rc.at[0], p2sem.at[1], to)
    q_second(7)

    load_tr.wait()
    load_mask.wait()

    @pl.loop(0, STATES // BLOCK)
    def _(ib):
        for cb in range(4):
            jb = st * 4 + cb
            keep = jnp.maximum(mask[ib, jb], (ib == jb).astype(jnp.int32)).astype(F32)
            at_rows = pl.ds(pl.multiple_of(ib * BLOCK, BLOCK), BLOCK)
            at_cols = pl.ds(cb * BLOCK, BLOCK)
            am[at_rows, at_cols] = (tr[at_rows, at_cols].astype(F32) * keep).astype(BF16)

    owner = x // 2
    quarter = x % 2
    mine = c == owner
    qcols = pl.ds(pl.multiple_of(x * 128, 128), 128)
    handed = []
    for n, (dx, dl) in enumerate(((0, 0), (0, 1), (1, 0), (3, 0), (2, 0), (1, 1), (3, 1), (2, 1))):
        who = sat(dx, dl)
        if n > 1:
            arrive(fg.at[who], f1sem.at[who])
        src = fg.at[who, :, qcols]
        dst = fr.at[quarter, tm]
        to = who * 2 + owner
        i = len(sends)
        sends.append(None)
        cp = pltpu.make_async_remote_copy(src, dst, ssem.at[i], f2sem.at[tm], device_id=(to, st), device_id_type=MESH)
        pl.when(to == tm)(pltpu.make_async_copy(src, dst, f2sem.at[tm]).start)
        pl.when(to != tm)(cp.start)
        handed.append((to, cp))
        part = jnp.dot(fg[who], am[pl.ds(pl.multiple_of(who * 512, 512), 512), :], preferred_element_type=F32)
        car[...] = part if n == 0 else car[...] + part
    send(car.at[pl.ds(rows - 8, 8), :], tail, tailsem.at[0], (nxt, st))

    load_bw.wait()
    load_rt.wait()
    load_ew.wait()
    value = p_sum(7)
    arrive(p2r.at[0], p2sem.at[0])
    arrive(p2rc.at[0], p2sem.at[1])
    p_drive = value + decode(p2r[0], p2rc[0])
    q_drive = acc[7, :, half:]
    for dy in YS:
        i = dy - 1
        arrive(q2r.at[i], q2sem.at[0, i])
        arrive(q2rc.at[i], q2sem.at[1, i])
        q_drive = q_drive + decode(q2r[i], q2rc[i])
    arrive(tail, tailsem.at[0])
    at_top = lax.broadcasted_iota(jnp.int32, (rows, half), 0) == 0
    is_edge = jnp.logical_and(lax.broadcasted_iota(jnp.int32, (rows, half), 0) == 0, tm == 0)
    ahead = []
    total = jnp.zeros((rows, 1), F32)
    for h, drive_sum in enumerate((p_drive, q_drive)):
        cols = slice(h * half, (h + 1) * half)
        term = jnp.exp(drive_sum - rt[:, cols]) * bw[:, cols]
        term = jnp.where(is_edge, jnp.broadcast_to(ew[:, cols], (rows, half)), term)
        acc[0, :, cols] = term
        carried = jnp.where(at_top, jnp.broadcast_to(tail[7:8, cols], (rows, half)), pltpu.roll(car[:, cols], 1, 0))
        total = total + jnp.sum(term * carried, axis=1, keepdims=True)
    tcol[pl.ds(0, rows), :] = jnp.broadcast_to(total, (rows, 128))
    tcol[pl.ds(rows, 256 - rows), :] = jnp.ones((256 - rows, 128), F32)
    tot[st] = tcol[...].T[0:8, :]
    for dx, dl in ((2, 1), (2, 0), (1, 1), (3, 1), (1, 0), (3, 0), (0, 1)):
        send(tot.at[st], tot.at[st], totsem.at[st], (tm, sat(dx, dl)))

    @pl.when(mine)
    def _():
        pltpu.make_async_copy(fr.at[quarter, tm], fr.at[quarter, tm], f2sem.at[tm]).wait()
        for dy, dz in STEPS:
            for dc in range(2):
                if (dy, dz, dc) != (0, 0, 0):
                    arrive(fr.at[quarter, at(dy, dz, dc)], f2sem.at[at(dy, dz, dc)])
        for dx in (1, 3, 2):
            pltpu.make_async_remote_copy(fr.at[quarter], fr.at[quarter], f3sem.at[0, dx], f3sem.at[1, quarter],
                                         device_id=(tm, sat(dx)), device_id_type=MESH).start()

    for dx in range(4):
        for dl in range(2):
            if (dx, dl) != (0, 0):
                who = sat(dx, dl)
                arrive(tot.at[who], totsem.at[who])
    sums = tot[0]
    for b in range(1, 8):
        sums = sums + tot[b]
    tsum[...] = sums
    tcol[...] = jnp.broadcast_to(sums[0:1, :], (128, 256)).T
    norm = tcol[pl.ds(0, rows), :]
    for h in range(2):
        for q in range(2):
            cols = pl.ds(h * half + q * 128, 128)
            w[h, tm, :, pl.ds(q * 128, 128)] = (acc[0, :, cols] / norm).astype(BF16)

    def w_send(h, who, dy, dz, dc=0):
        send(w.at[h, who], w.at[h, who], (coresem if dc else wsem).at[h, who], (at(dy, dz, dc), st))

    def w_arrive(h, who, dc=0):
        arrive(w.at[h, who], (coresem if dc else wsem).at[h, who])

    w_send(0, tm, 0, 1)
    for dy in YS:
        w_send(1, tm, dy, 0)
    for dy in YS:
        w_send(0, tm, dy, 0)
    w_send(1, tm, 0, 1)
    w_send(0, tm, 0, 0, 1)
    w_send(1, tm, 0, 0, 1)
    send(tsum, first, firstsem.at[0], (prev, st))
    opp = at(0, 1)
    w_arrive(0, opp)
    for dy in YS:
        w_send(0, opp, dy, 0)
    w_send(0, opp, 0, 0, 1)
    for dy in (1, 3, 2):
        who = at(dy, 0)
        w_arrive(1, who)
        w_send(1, who, 0, 1)
        w_send(1, who, 0, 0, 1)
    for dy in (1, 3, 2):
        who = at(dy, 0)
        w_arrive(0, who)
        w_send(0, who, 0, 0, 1)
    w_arrive(1, opp)
    w_send(1, opp, 0, 0, 1)
    for dy in (1, 3, 2):
        for h in (0, 1):
            who = at(dy, 1)
            w_arrive(h, who)
            w_send(h, who, 0, 0, 1)

    arrive(first, firstsem.at[0])
    lanes = lax.broadcasted_iota(jnp.int32, (8, 256), 1)
    here = pltpu.roll(tsum[...], 255, 1)
    there = jnp.broadcast_to(first[...][:, 0:1], (8, 256))
    loglik[...] = jnp.log(jnp.where(lanes == rows - 1, there, here))

    for q in range(2):
        @pl.when(jnp.logical_not(jnp.logical_and(mine, quarter == q)))
        def _(q=q):
            pltpu.make_async_remote_copy(fr.at[q], fr.at[q], f3sem.at[0, 0], f3sem.at[1, q], device_id=(tm, st), device_id_type=MESH).wait_recv()
        lt[pl.ds(q * 128, 128), :] = pltpu.roll(fr[q].reshape(16 * rows, 128).astype(F32), 1, 0).T.astype(BF16)
    at_rows = pl.ds(pl.multiple_of(tm * 256, 256), 256)
    scale = STATES * STATES / time_total
    for h in range(2):
        for dy, dz in STEPS:
            w_arrive(h, at(dy, dz, 1), 1)
        pair = jnp.dot(lt[...], w[h].reshape(16 * rows, half), preferred_element_type=F32)
        at_cols = pl.ds(h * half, half)
        out[:, at_cols] = am[at_rows, at_cols].astype(F32) * pair * scale
    store = local(out, counts, 14)

    for i, cp in enumerate(sends):
        if cp is not None:
            cp.wait_send()
    for to, cp in handed:
        pl.when(to != tm)(cp.wait_send)

    @pl.when(mine)
    def _():
        for dx in (1, 3, 2):
            pltpu.make_async_remote_copy(fr.at[quarter], fr.at[quarter], f3sem.at[0, dx], f3sem.at[1, quarter],
                                         device_id=(tm, sat(dx)), device_id_type=MESH).wait_send()
    store.wait()


def place(counts, loglik, counts_out, loglik_out):
    counts_out[...] = counts[...]
    loglik_out[...] = loglik[0, 0:loglik_out.shape[0]]


def shards(spikes, log_rate, forward, backward, transition, rate_total, edge_weight, block_mask):
    rows = forward.shape[0]
    time_total = spikes.shape[0]
    neurons, width = log_rate.shape
    vm = pltpu.VMEM
    dma = pltpu.SemaphoreType.DMA
    scratch = [
        pltpu.SMEM(block_mask.shape, jnp.int32), vm((256, 16 * rows), BF16), vm((8, 2 * rows, neurons), jnp.int32), vm((neurons, width), BF16), vm((rows, width), BF16), vm((rows, width), F32),
        vm((STATES, width), BF16), vm((STATES, width), BF16), vm((1, width), F32), vm((1, width), F32), vm((256, width), F32),
        vm((8, width), F32), vm((8, rows, width), BF16), vm((2, 16, rows, 128), BF16),
        vm((8, rows, width), F32), vm((8, rows, width), F32), vm((8, rows, width), F32),
    ]
    for n in (6, 4, 3, 1):
        scratch += [vm((n, rows, 256), I16), vm((n, rows, 256), I16), vm((n, 8, 256), F32), vm((n, 8, 256), F32)]
    scratch += [
        vm((rows, width), F32), vm((256, 128), F32), vm((8, 8, 256), F32), vm((8, 256), F32), vm((8, 256), F32), vm((2, 16, rows, 256), BF16),
        dma((20,)), dma((120,)), dma((8,)), dma((1,)), dma((8,)), dma((16,)), dma((2, 4)), dma((2, 6)), dma((2, 4)), dma((2, 3)), dma((2,)),
        dma((8,)), dma((1,)), dma((2, 16)), dma((2, 16)),
    ]
    hbm = pl.BlockSpec(memory_space=pl.ANY)
    counts, loglik = pl.pallas_call(
        functools.partial(kernel, time_total),
        out_shape=(jax.ShapeDtypeStruct((256, width), F32), jax.ShapeDtypeStruct((8, 256), F32)),
        in_specs=[hbm] * 8,
        out_specs=(hbm, pl.BlockSpec(memory_space=pltpu.VMEM)),
        scratch_shapes=scratch,
        compiler_params=pltpu.CompilerParams(collective_id=0, has_side_effects=True, vmem_limit_bytes=56 * 2**20),
    )(spikes, log_rate, forward, backward, transition, rate_total.reshape(1, width), edge_weight.reshape(1, width), block_mask)
    return pl.pallas_call(
        place,
        out_shape=(jax.ShapeDtypeStruct((256, width), F32), jax.ShapeDtypeStruct((rows,), F32)),
    )(counts, loglik)


def solution(mesh):
    in_specs = (P(None, "tm"), P("tm", "state"), P("tm", "state"), P("tm", "state"), P(None, "state"), P("state"), P("state"), P())
    out_specs = (P("tm", "state"), P("tm"))
    return jax.shard_map(shards, mesh=mesh, in_specs=in_specs, out_specs=out_specs, check_vma=False)
```

```python
import functools
import jax
import jax.numpy as jnp
from jax import lax
from jax.experimental import pallas as pl
from jax.experimental.pallas import tpu as pltpu
from jax.sharding import PartitionSpec as P

MESH = pl.DeviceIdType.MESH
STATES = 4096
BLOCK = 128
F32, BF16, I16 = jnp.float32, jnp.bfloat16, jnp.int16
TOP = 32760.0
ROUND = 12582912.0
STEPS = ((2, 1), (1, 1), (3, 1), (0, 1), (2, 0), (1, 0), (3, 0), (0, 0))
YS = (2, 1, 3)
EARLY = 3
RELAY = 4


def encode(value):
    most = jnp.maximum(jnp.max(jnp.abs(value), axis=0, keepdims=True), 1e-30)
    coded = (value * (TOP / most) + ROUND) - ROUND
    return coded.astype(jnp.int32).astype(I16), jnp.broadcast_to(most * (1.0 / TOP), (8, value.shape[1]))


def decode(coded, scale):
    return coded.astype(jnp.int32).astype(F32) * scale[0:1, :]


def kernel(time_total, spikes, log_rate, forward, backward, transition, rate, edge, block_mask,
           counts, loglik,
           mask, lt, spk, lr, fw, bw, tr, am, rt, ew,
           fg, fr, cs, cr, acc,
           p1s, p1r, p1sc, p1rc, q1s, q1r, q1sc, q1rc, q2s, q2r, q2sc, q2rc, p2s, p2r, p2sc, p2rc,
           car, tcol, tot, tsum, first, w,
           lsem, ssem, csem, tailsem, f1sem, f1tsem, handsem, f2sem, f3sem, p1sem, q1sem, q2sem, p2sem, totsem, firstsem, wsem, coresem):
    tm, st = lax.axis_index("tm"), lax.axis_index("state")
    y, zh, c = tm // 4, (tm // 2) % 2, tm % 2
    zl, x = st // 4, st % 4

    def at(dy=0, dz=0, dc=0):
        return (((y + dy) % 4) * 2 + (zh + dz) % 2) * 2 + (c + dc) % 2

    def sat(dx=0, dl=0):
        return ((zl + dl) % 2) * 4 + (x + dx) % 4

    rows = fw.shape[0]
    group = 2 * rows
    half = 256

    def local(src, dst, i):
        cp = pltpu.make_async_copy(src, dst, lsem.at[i])
        cp.start()
        return cp

    def spike_load(s):
        dy, dz = STEPS[s]
        row = pl.multiple_of((((y + dy) % 4) * 2 + (zh + dz) % 2) * group, group)
        return local(spikes.at[pl.ds(row, group), :], spk.at[s % spk.shape[0]], s % spk.shape[0])

    loads = {}
    load_fw = local(forward, fw, 8)
    load_lr = local(log_rate, lr, 9)
    for s in range(spk.shape[0]):
        loads[s] = spike_load(s)
    load_tr = local(transition, tr, 10)
    load_mask = local(block_mask, mask, 15)
    load_bw = local(backward, bw, 11)
    load_rt = local(rate, rt, 12)
    load_ew = local(edge, ew, 13)

    barrier = pltpu.get_barrier_semaphore()
    prev, nxt = (tm + 15) % 16, (tm + 1) % 16
    peers = [(at(dc=1), st)] + [(at(dy, dz, dc), st) for dy in range(4) for dz in range(2) for dc in range(2) if (dy != 0) != (dz != 0)]
    peers += [(tm, sat(dx, dl)) for dx in range(4) for dl in range(2) if (dx, dl) != (0, 0)]
    peers += [(prev, st), (nxt, st)]
    for peer in peers:
        pl.semaphore_signal(barrier, inc=1, device_id=peer, device_id_type=MESH)

    def send(src, dst, i, rsem, device):
        pltpu.make_async_remote_copy(src, dst, ssem.at[i], rsem, device_id=device, device_id_type=MESH).start()

    def sent(ref, i):
        pltpu.make_async_remote_copy(ref, ref, ssem.at[i], ssem.at[i], device_id=(tm, st), device_id_type=MESH).wait_send()

    def arrive(dst, rsem):
        pltpu.make_async_remote_copy(dst, dst, ssem.at[0], rsem, device_id=(tm, st), device_id_type=MESH).wait_recv()


    def drive(s):
        loads[s].wait()
        part = jnp.dot(spk[s % spk.shape[0]].astype(F32).astype(BF16), lr[...], preferred_element_type=F32)
        parts = part.reshape(2, rows, 512)
        acc[s] = jnp.where(c == 0, parts[0], parts[1])
        cs[s] = jnp.where(c == 0, parts[1], parts[0])
        if s + spk.shape[0] < 8:
            loads[s + spk.shape[0]] = spike_load(s + spk.shape[0])

    def swap(s):
        send(cs.at[s], cr.at[s], 0, csem.at[s], (at(dc=1), st))

    def pair_up(s):
        dy, dz = STEPS[s]
        arrive(cr.at[s], csem.at[s])
        if dy != 0:
            i = dz * 3 + dy - 1
            p1s[i], p1sc[i] = encode(acc[s, :, 0:half] + cr[s, :, 0:half])
            to = (at(dy), st)
            send(p1s.at[i], p1r.at[i], 4, p1sem.at[0, i], to)
            send(p1sc.at[i], p1rc.at[i], 5, p1sem.at[1, i], to)
        else:
            acc[s, :, 0:half] += cr[s, :, 0:half]
        if dz != 0:
            q1s[dy], q1sc[dy] = encode(acc[s, :, half:] + cr[s, :, half:])
            to = (at(0, 1), st)
            send(q1s.at[dy], q1r.at[dy], 6, q1sem.at[0, dy], to)
            send(q1sc.at[dy], q1rc.at[dy], 7, q1sem.at[1, dy], to)
        else:
            acc[s, :, half:] += cr[s, :, half:]

    def q_second(s):
        dy, _ = STEPS[s]
        arrive(q1r.at[dy], q1sem.at[0, dy])
        arrive(q1rc.at[dy], q1sem.at[1, dy])
        value = acc[s, :, half:] + decode(q1r[dy], q1rc[dy])
        if dy == 0:
            acc[s, :, half:] = value
        else:
            i = dy - 1
            q2s[i], q2sc[i] = encode(value)
            to = (at(dy), st)
            send(q2s.at[i], q2r.at[i], 8, q2sem.at[0, i], to)
            send(q2sc.at[i], q2rc.at[i], 9, q2sem.at[1, i], to)

    def p_sum(s):
        dz = STEPS[s][1]
        value = acc[s, :, 0:half]
        for dy in YS:
            i = dz * 3 + dy - 1
            arrive(p1r.at[i], p1sem.at[0, i])
            arrive(p1rc.at[i], p1sem.at[1, i])
            value = value + decode(p1r[i], p1rc[i])
        return value

    own = pl.ds(16, rows)
    head = pl.ds(0, 16)

    def spread(who, dx, dl):
        send(fg.at[who, own], fg.at[who, own], 1, f1sem.at[who], (tm, sat(dx, dl)))

    load_fw.wait()
    fg[st, 16:16 + rows, :] = fw[...]
    load_lr.wait()
    drive(0)
    pl.semaphore_wait(barrier, len(peers))
    swap(0)
    send(fg.at[st, pl.ds(rows, 16)], fg.at[st, head], 3, tailsem.at[0], (nxt, st))
    spread(st, 0, 1)
    for dx in (1, 3, 2):
        spread(st, dx, 0)
    other = sat(0, 1)
    for s in range(8):
        if s < 7:
            drive(s + 1)
            swap(s + 1)
        pair_up(s)
        if s == 3:
            arrive(fg.at[st, head], tailsem.at[0])
            for dx in range(4):
                for dl in range(2):
                    if (dx, dl) != (0, 0):
                        send(fg.at[st, head], fg.at[st, head], 2, f1tsem.at[0], (tm, sat(dx, dl)))
        if s == RELAY:
            arrive(fg.at[other, own], f1sem.at[other])
            for dx in (1, 3, 2):
                spread(other, dx, 0)

    load_tr.wait()
    load_mask.wait()

    @pl.loop(0, STATES // BLOCK)
    def _(ib):
        for cb in range(4):
            jb = st * 4 + cb
            keep = jnp.maximum(mask[ib, jb], (ib == jb).astype(jnp.int32)).astype(F32)
            at_rows = pl.ds(pl.multiple_of(ib * BLOCK, BLOCK), BLOCK)
            at_cols = pl.ds(cb * BLOCK, BLOCK)
            am[at_rows, at_cols] = (tr[at_rows, at_cols].astype(F32) * keep).astype(BF16)

    q_second(4)
    q_second(5)
    q_second(6)
    value = p_sum(3)
    p2s[0], p2sc[0] = encode(value)
    to = (at(0, 1), st)
    send(p2s.at[0], p2r.at[0], 10, p2sem.at[0], to)
    send(p2sc.at[0], p2rc.at[0], 11, p2sem.at[1], to)
    q_second(7)

    owner = x // 2
    quarter = x % 2
    mine = c == owner
    qcols = pl.ds(pl.multiple_of(x * 128, 128), 128)
    handed = []
    arrive(fg.at[pl.ds(0, 7), head], f1tsem.at[0])
    for n, (dx, dl) in enumerate(((0, 0), (0, 1), (1, 0), (3, 0), (2, 0), (1, 1), (3, 1), (2, 1))):
        who = sat(dx, dl)
        if n > 1:
            arrive(fg.at[who, own], f1sem.at[who])
        src = fg.at[who, own, qcols]
        dst = fr.at[quarter, tm]
        to = who * 2 + owner
        cp = pltpu.make_async_remote_copy(src, dst, handsem.at[n], f2sem.at[0], device_id=(to, st), device_id_type=MESH)
        pl.when(to == tm)(pltpu.make_async_copy(src, dst, f2sem.at[1]).start)
        pl.when(to != tm)(cp.start)
        handed.append((to, cp))
        part = jnp.dot(fg[who], am[pl.ds(pl.multiple_of(who * 512, 512), 512), :], preferred_element_type=F32)
        car[...] = part if n == 0 else car[...] + part
    load_bw.wait()
    load_rt.wait()
    load_ew.wait()
    value = p_sum(7)
    arrive(p2r.at[0], p2sem.at[0])
    arrive(p2rc.at[0], p2sem.at[1])
    p_drive = value + decode(p2r[0], p2rc[0])
    q_drive = acc[7, :, half:]
    for dy in YS:
        i = dy - 1
        arrive(q2r.at[i], q2sem.at[0, i])
        arrive(q2rc.at[i], q2sem.at[1, i])
        q_drive = q_drive + decode(q2r[i], q2rc[i])
    moved = pltpu.roll(car[...], 1, 0)
    is_edge = jnp.logical_and(lax.broadcasted_iota(jnp.int32, (rows, half), 0) == 0, tm == 0)
    ahead = []
    total = jnp.zeros((rows, 1), F32)
    for h, drive_sum in enumerate((p_drive, q_drive)):
        cols = slice(h * half, (h + 1) * half)
        term = jnp.exp(drive_sum - rt[:, cols]) * bw[:, cols]
        term = jnp.where(is_edge, jnp.broadcast_to(ew[:, cols], (rows, half)), term)
        acc[0, :, cols] = term
        carried = moved[16:, cols]
        total = total + jnp.sum(term * carried, axis=1, keepdims=True)
    tcol[pl.ds(0, rows), :] = jnp.broadcast_to(total, (rows, 128))
    tcol[pl.ds(rows, 256 - rows), :] = jnp.ones((256 - rows, 128), F32)
    tot[st] = tcol[...].T[0:8, :]
    for dx, dl in ((2, 1), (2, 0), (1, 1), (3, 1), (1, 0), (3, 0), (0, 1)):
        send(tot.at[st], tot.at[st], 12, totsem.at[0], (tm, sat(dx, dl)))

    def hand_on(q, n, dx, i):
        part = fr.at[q, pl.ds(8 * n, 8)]
        return pltpu.make_async_remote_copy(part, part, ssem.at[i], f3sem.at[2 * q + n], device_id=(tm, sat(dx)), device_id_type=MESH)

    def handed_part(q, n):
        arrive(fr.at[q, pl.ds(8 * n, 8)], f3sem.at[2 * q + n])

    @pl.when(mine)
    def _():
        pltpu.make_async_copy(fr.at[quarter, tm], fr.at[quarter, tm], f2sem.at[1]).wait()
        arrive(fr.at[quarter, pl.ds(0, 15)], f2sem.at[0])
        hand_on(quarter, 0, 1, 16).start()
        hand_on(quarter, 1, 3, 17).start()
        hand_on(quarter, 1, 1, 18).start()
        hand_on(quarter, 0, 3, 19).start()

    arrive(tot.at[pl.ds(0, 7)], totsem.at[0])
    sums = tot[0]
    for b in range(1, 8):
        sums = sums + tot[b]
    tsum[...] = sums
    tcol[...] = jnp.broadcast_to(sums[0:1, :], (128, 256)).T
    norm = tcol[pl.ds(0, rows), :]
    for h in range(2):
        for q in range(2):
            cols = pl.ds(h * half + q * 128, 128)
            w[h, c, tm // 2, :, pl.ds(q * 128, 128)] = (acc[0, :, cols] / norm).astype(BF16)

    def w_send(h, who, dy, dz, dc=0):
        send(w.at[h, c, who // 2], w.at[h, c, who // 2], 14 + h, coresem.at[h] if dc else wsem.at[h, who // 2], (at(dy, dz, dc), st))

    def w_arrive(h, who):
        arrive(w.at[h, c, who // 2], wsem.at[h, who // 2])

    w_send(0, tm, 0, 1)
    for dy in YS:
        w_send(1, tm, dy, 0)
    for dy in YS:
        w_send(0, tm, dy, 0)
    w_send(1, tm, 0, 1)
    w_send(0, tm, 0, 0, 1)
    w_send(1, tm, 0, 0, 1)
    send(tsum, first, 13, firstsem.at[0], (prev, st))

    opp = at(0, 1)
    w_arrive(0, opp)
    for dy in YS:
        w_send(0, opp, dy, 0)
    w_send(0, opp, 0, 0, 1)
    for dy in (1, 3, 2):
        who = at(dy, 0)
        w_arrive(1, who)
        w_send(1, who, 0, 1)
        w_send(1, who, 0, 0, 1)
    for q in range(2):
        away = (x + 4 - 2 * c - q) % 4

        @pl.when(away == 1)
        def _(q=q):
            handed_part(q, 0)
            hand_on(q, 0, 1, 20).start()

        @pl.when(away == 3)
        def _(q=q):
            handed_part(q, 1)
            hand_on(q, 1, 3, 20).start()

    for dy in (1, 3, 2):
        who = at(dy, 0)
        w_arrive(0, who)
        w_send(0, who, 0, 0, 1)
    w_arrive(1, opp)
    w_send(1, opp, 0, 0, 1)
    for dy in (1, 3):
        for h in (0, 1):
            who = at(dy, 1)
            w_arrive(h, who)
            w_send(h, who, 0, 0, 1)
    arrive(first, firstsem.at[0])
    lanes = lax.broadcasted_iota(jnp.int32, (8, 256), 1)
    here = pltpu.roll(tsum[...], 255, 1)
    there = jnp.broadcast_to(first[...][:, 0:1], (8, 256))
    loglik[...] = jnp.log(jnp.where(lanes == rows - 1, there, here))
    for h in (0, 1):
        who = at(2, 1)
        w_arrive(h, who)
        w_send(h, who, 0, 0, 1)
    for q in range(2):
        away = (x + 4 - 2 * c - q) % 4
        pl.when(jnp.logical_or(away == 2, away == 3))(functools.partial(handed_part, q, 0))
        pl.when(jnp.logical_or(away == 2, away == 1))(functools.partial(handed_part, q, 1))
        later = pltpu.roll(fr[q].reshape(16 * rows, 128).astype(F32), 1, 0).reshape(8, 2, rows, 128)
        for k in range(2):
            lt[k, pl.ds(q * 128, 128), :] = later[:, k].reshape(8 * rows, 128).T.astype(BF16)
    at_rows = pl.ds(pl.multiple_of(tm * 256, 256), 256)
    scale = STATES * STATES / time_total
    pair = [jnp.dot(lt[c], w[h, c].reshape(8 * rows, half), preferred_element_type=F32) for h in range(2)]
    for h in range(2):
        arrive(w.at[h, 1 - c], coresem.at[h])
        both = pair[h] + jnp.dot(lt[1 - c], w[h, 1 - c].reshape(8 * rows, half), preferred_element_type=F32)
        at_cols = pl.ds(h * half, half)
        counts[:, at_cols] = am[at_rows, at_cols].astype(F32) * both * scale

    sent(cs, 0)
    sent(fg.at[pl.ds(0, 7), own], 1)
    sent(fg.at[pl.ds(0, 7), head], 2)
    sent(fg.at[0, head], 3)
    for i, ref in enumerate((p1s, p1sc, q1s, q1sc, q2s, q2sc, p2s, p2sc)):
        sent(ref, 4 + i)
    sent(tot.at[pl.ds(0, 7)], 12)
    sent(tsum, 13)
    for h in range(2):
        sent(w.at[h, 0], 14 + h)
        sent(w.at[h, 1, pl.ds(0, 7)], 14 + h)
    for to, cp in handed:
        pl.when(to != tm)(cp.wait_send)

    @pl.when(mine)
    def _():
        for n, (m, dx) in enumerate(((0, 1), (1, 3), (1, 1), (0, 3))):
            hand_on(quarter, m, dx, 16 + n).wait_send()

    sent(fr.at[0, pl.ds(0, 8)], 20)


def place(counts, loglik, counts_out, loglik_out):
    counts_out[...] = counts[...]
    loglik_out[...] = loglik[0, 0:loglik_out.shape[0]]


def shards(spikes, log_rate, forward, backward, transition, rate_total, edge_weight, block_mask):
    rows = forward.shape[0]
    time_total = spikes.shape[0]
    neurons, width = log_rate.shape
    vm = pltpu.VMEM
    dma = pltpu.SemaphoreType.DMA
    scratch = [
        pltpu.SMEM(block_mask.shape, jnp.int32), vm((2, 256, 8 * rows), BF16), vm((8, 2 * rows, neurons), jnp.int32), vm((neurons, width), BF16), vm((rows, width), BF16), vm((rows, width), F32),
        vm((STATES, width), BF16), vm((STATES, width), BF16), vm((1, width), F32), vm((1, width), F32),
        vm((8, 16 + rows, width), BF16), vm((2, 16, rows, 128), BF16),
        vm((8, rows, width), F32), vm((8, rows, width), F32), vm((8, rows, width), F32),
    ]
    for n in (6, 4, 3, 1):
        scratch += [vm((n, rows, 256), I16), vm((n, rows, 256), I16), vm((n, 8, 256), F32), vm((n, 8, 256), F32)]
    scratch += [
        vm((16 + rows, width), F32), vm((256, 128), F32), vm((8, 8, 256), F32), vm((8, 256), F32), vm((8, 256), F32), vm((2, 2, 8, rows, 256), BF16),
        dma((16,)), dma((21,)), dma((8,)), dma((1,)), dma((8,)), dma((1,)), dma((8,)), dma((2,)), dma((4,)),
        dma((2, 6)), dma((2, 4)), dma((2, 3)), dma((2,)), dma((1,)), dma((1,)), dma((2, 8)), dma((2,)),
    ]
    hbm = pl.BlockSpec(memory_space=pl.ANY)
    counts, loglik = pl.pallas_call(
        functools.partial(kernel, time_total),
        out_shape=(vm((256, width), F32), vm((8, 256), F32)),
        in_specs=[hbm] * 8,
        out_specs=(pl.BlockSpec(memory_space=pltpu.VMEM), pl.BlockSpec(memory_space=pltpu.VMEM)),
        scratch_shapes=scratch,
        compiler_params=pltpu.CompilerParams(collective_id=0, has_side_effects=True, vmem_limit_bytes=56 * 2**20),
    )(spikes, log_rate, forward, backward, transition, rate_total.reshape(1, width), edge_weight.reshape(1, width), block_mask)
    return pl.pallas_call(
        place,
        out_shape=(jax.ShapeDtypeStruct((256, width), F32), jax.ShapeDtypeStruct((rows,), F32)),
    )(pltpu.with_memory_space_constraint(counts, pltpu.VMEM), pltpu.with_memory_space_constraint(loglik, pltpu.VMEM))


def solution(mesh):
    in_specs = (P(None, "tm"), P("tm", "state"), P("tm", "state"), P("tm", "state"), P(None, "state"), P("state"), P("state"), P())
    out_specs = (P("tm", "state"), P("tm"))
    return jax.shard_map(shards, mesh=mesh, in_specs=in_specs, out_specs=out_specs, check_vma=False)
```

```python
import functools
import jax
import jax.numpy as jnp
from jax import lax
from jax.experimental import pallas as pl
from jax.experimental.pallas import tpu as pltpu
from jax.sharding import PartitionSpec as P

MESH = pl.DeviceIdType.MESH
STATES = 4096
BLOCK = 128
F32, BF16, I16 = jnp.float32, jnp.bfloat16, jnp.int16
TOP = 32760.0
ROUND = 12582912.0
STEPS = ((2, 1), (1, 1), (3, 1), (0, 1), (2, 0), (1, 0), (3, 0), (0, 0))
YS = (2, 1, 3)
EARLY = 3
RELAY = 3


def encode(value):
    most = jnp.maximum(jnp.max(jnp.abs(value), axis=0, keepdims=True), 1e-30)
    coded = (value * (TOP / most) + ROUND) - ROUND
    return coded.astype(jnp.int32).astype(I16), jnp.broadcast_to(most * (1.0 / TOP), (8, value.shape[1]))


def decode(coded, scale):
    return coded.astype(jnp.int32).astype(F32) * scale[0:1, :]


def kernel(time_total, spikes, log_rate, forward, backward, transition, rate, edge, block_mask,
           counts, loglik,
           mask, lt, spk, lr, fw, bw, tr, am, rt, ew, pair,
           fg, fr, cs, cr, acc,
           p1s, p1r, p1sc, p1rc, q1s, q1r, q1sc, q1rc, q2s, q2r, q2sc, q2rc, p2s, p2r, p2sc, p2rc,
           car, tcol, tot, tsum, first, w,
           lsem, ssem, csem, tailsem, f1sem, f1tsem, handsem, f2sem, f3sem, p1sem, q1sem, q2sem, p2sem, totsem, firstsem, wsem, coresem):
    tm, st = lax.axis_index("tm"), lax.axis_index("state")
    y, zh, c = tm // 4, (tm // 2) % 2, tm % 2
    zl, x = st // 4, st % 4

    def at(dy=0, dz=0, dc=0):
        return (((y + dy) % 4) * 2 + (zh + dz) % 2) * 2 + (c + dc) % 2

    def sat(dx=0, dl=0):
        return ((zl + dl) % 2) * 4 + (x + dx) % 4

    rows = fw.shape[0]
    group = 2 * rows
    half = 256

    def local(src, dst, i):
        cp = pltpu.make_async_copy(src, dst, lsem.at[i])
        cp.start()
        return cp

    def spike_load(s):
        dy, dz = STEPS[s]
        row = pl.multiple_of((((y + dy) % 4) * 2 + (zh + dz) % 2) * group, group)
        return local(spikes.at[pl.ds(row, group), :], spk.at[s % spk.shape[0]], s % spk.shape[0])

    loads = {}
    load_fw = local(forward, fw, 8)
    load_lr = local(log_rate, lr, 9)
    for s in range(spk.shape[0]):
        loads[s] = spike_load(s)
    load_tr = local(transition, tr, 10)
    load_mask = local(block_mask, mask, 15)
    load_bw = local(backward, bw, 11)
    load_rt = local(rate, rt, 12)
    load_ew = local(edge, ew, 13)

    barrier = pltpu.get_barrier_semaphore()
    prev, nxt = (tm + 15) % 16, (tm + 1) % 16
    peers = [(at(dc=1), st)] + [(at(dy, dz, dc), st) for dy in range(4) for dz in range(2) for dc in range(2) if (dy != 0) != (dz != 0)]
    peers += [(tm, sat(dx, dl)) for dx in range(4) for dl in range(2) if (dx, dl) != (0, 0)]
    peers += [(prev, st), (nxt, st)]
    for peer in peers:
        pl.semaphore_signal(barrier, inc=1, device_id=peer, device_id_type=MESH)

    def send(src, dst, i, rsem, device):
        pltpu.make_async_remote_copy(src, dst, ssem.at[i], rsem, device_id=device, device_id_type=MESH).start()

    def sent(ref, i):
        pltpu.make_async_remote_copy(ref, ref, ssem.at[i], ssem.at[i], device_id=(tm, st), device_id_type=MESH).wait_send()

    def arrive(dst, rsem):
        pltpu.make_async_remote_copy(dst, dst, ssem.at[0], rsem, device_id=(tm, st), device_id_type=MESH).wait_recv()


    def drive(s):
        loads[s].wait()
        part = jnp.dot(spk[s % spk.shape[0]].astype(F32).astype(BF16), lr[...], preferred_element_type=F32)
        parts = part.reshape(2, rows, 512)
        acc[s] = jnp.where(c == 0, parts[0], parts[1])
        cs[s] = jnp.where(c == 0, parts[1], parts[0])
        if s + spk.shape[0] < 8:
            loads[s + spk.shape[0]] = spike_load(s + spk.shape[0])

    def swap(s):
        send(cs.at[s], cr.at[s], 0, csem.at[s], (at(dc=1), st))

    def pair_up(s):
        dy, dz = STEPS[s]
        arrive(cr.at[s], csem.at[s])
        if dy != 0:
            i = dz * 3 + dy - 1
            p1s[i], p1sc[i] = encode(acc[s, :, 0:half] + cr[s, :, 0:half])
            to = (at(dy), st)
            send(p1s.at[i], p1r.at[i], 4, p1sem.at[0, i], to)
            send(p1sc.at[i], p1rc.at[i], 5, p1sem.at[1, i], to)
        else:
            acc[s, :, 0:half] += cr[s, :, 0:half]
        if dz != 0:
            q1s[dy], q1sc[dy] = encode(acc[s, :, half:] + cr[s, :, half:])
            to = (at(0, 1), st)
            send(q1s.at[dy], q1r.at[dy], 6, q1sem.at[0, dy], to)
            send(q1sc.at[dy], q1rc.at[dy], 7, q1sem.at[1, dy], to)
        else:
            acc[s, :, half:] += cr[s, :, half:]

    def q_second(s):
        dy, _ = STEPS[s]
        arrive(q1r.at[dy], q1sem.at[0, dy])
        arrive(q1rc.at[dy], q1sem.at[1, dy])
        value = acc[s, :, half:] + decode(q1r[dy], q1rc[dy])
        if dy == 0:
            acc[s, :, half:] = value
        else:
            i = dy - 1
            q2s[i], q2sc[i] = encode(value)
            to = (at(dy), st)
            send(q2s.at[i], q2r.at[i], 8, q2sem.at[0, i], to)
            send(q2sc.at[i], q2rc.at[i], 9, q2sem.at[1, i], to)

    def p_sum(s):
        dz = STEPS[s][1]
        value = acc[s, :, 0:half]
        for dy in YS:
            i = dz * 3 + dy - 1
            arrive(p1r.at[i], p1sem.at[0, i])
            arrive(p1rc.at[i], p1sem.at[1, i])
            value = value + decode(p1r[i], p1rc[i])
        return value

    own = pl.ds(16, rows)
    head = pl.ds(0, 16)

    def spread(who, dx, dl):
        send(fg.at[who, own], fg.at[who, own], 1, f1sem.at[who], (tm, sat(dx, dl)))

    load_fw.wait()
    fg[st, 16:16 + rows, :] = fw[...]
    load_lr.wait()
    drive(0)
    pl.semaphore_wait(barrier, len(peers))
    swap(0)
    send(fg.at[st, pl.ds(rows, 16)], fg.at[st, head], 3, tailsem.at[0], (nxt, st))
    spread(st, 0, 1)
    for dx in (1, 3, 2):
        spread(st, dx, 0)
    other = sat(0, 1)
    for s in range(8):
        if s < 7:
            drive(s + 1)
            swap(s + 1)
        pair_up(s)
        if s == 3:
            arrive(fg.at[st, head], tailsem.at[0])
            for dx in range(4):
                for dl in range(2):
                    if (dx, dl) != (0, 0):
                        send(fg.at[st, head], fg.at[st, head], 2, f1tsem.at[0], (tm, sat(dx, dl)))
        if s == RELAY:
            arrive(fg.at[other, own], f1sem.at[other])
            for dx in (1, 3, 2):
                spread(other, dx, 0)

    value = p_sum(3)
    p2s[0], p2sc[0] = encode(value)
    to = (at(0, 1), st)
    send(p2s.at[0], p2r.at[0], 10, p2sem.at[0], to)
    send(p2sc.at[0], p2rc.at[0], 11, p2sem.at[1], to)

    load_tr.wait()
    load_mask.wait()

    @pl.loop(0, STATES // BLOCK)
    def _(ib):
        for cb in range(4):
            jb = st * 4 + cb
            keep = jnp.maximum(mask[ib, jb], (ib == jb).astype(jnp.int32)).astype(F32)
            at_rows = pl.ds(pl.multiple_of(ib * BLOCK, BLOCK), BLOCK)
            at_cols = pl.ds(cb * BLOCK, BLOCK)
            am[at_rows, at_cols] = (tr[at_rows, at_cols].astype(F32) * keep).astype(BF16)

    q_second(4)
    q_second(5)
    q_second(6)
    q_second(7)

    owner = x // 2
    quarter = x % 2
    mine = c == owner
    qcols = pl.ds(pl.multiple_of(x * 128, 128), 128)
    handed = []
    arrive(fg.at[pl.ds(0, 7), head], f1tsem.at[0])
    for n, (dx, dl) in enumerate(((0, 0), (0, 1), (1, 0), (3, 0), (2, 0), (1, 1), (3, 1), (2, 1))):
        who = sat(dx, dl)
        if n > 1:
            arrive(fg.at[who, own], f1sem.at[who])
        src = fg.at[who, own, qcols]
        dst = fr.at[quarter, zh * 8 + y * 2 + c]
        to = who * 2 + owner
        cp = pltpu.make_async_remote_copy(src, dst, handsem.at[n], f2sem.at[zh], device_id=(to, st), device_id_type=MESH)
        pl.when(to == tm)(pltpu.make_async_copy(src, dst, f2sem.at[2]).start)
        pl.when(to != tm)(cp.start)
        handed.append((to, cp))
        part = jnp.dot(fg[who], am[pl.ds(pl.multiple_of(who * 512, 512), 512), :], preferred_element_type=F32)
        car[...] = part if n == 0 else car[...] + part
    load_bw.wait()
    load_rt.wait()
    load_ew.wait()
    value = p_sum(7)
    arrive(p2r.at[0], p2sem.at[0])
    arrive(p2rc.at[0], p2sem.at[1])
    p_drive = value + decode(p2r[0], p2rc[0])
    q_drive = acc[7, :, half:]
    for dy in YS:
        i = dy - 1
        arrive(q2r.at[i], q2sem.at[0, i])
        arrive(q2rc.at[i], q2sem.at[1, i])
        q_drive = q_drive + decode(q2r[i], q2rc[i])
    moved = pltpu.roll(car[...], 1, 0)
    is_edge = jnp.logical_and(lax.broadcasted_iota(jnp.int32, (rows, half), 0) == 0, tm == 0)
    ahead = []
    total = jnp.zeros((rows, 1), F32)
    for h, drive_sum in enumerate((p_drive, q_drive)):
        cols = slice(h * half, (h + 1) * half)
        term = jnp.exp(drive_sum - rt[:, cols]) * bw[:, cols]
        term = jnp.where(is_edge, jnp.broadcast_to(ew[:, cols], (rows, half)), term)
        acc[0, :, cols] = term
        carried = moved[16:, cols]
        total = total + jnp.sum(term * carried, axis=1, keepdims=True)
    tcol[pl.ds(0, rows), :] = jnp.broadcast_to(total, (rows, 128))
    tcol[pl.ds(rows, 256 - rows), :] = jnp.ones((256 - rows, 128), F32)
    tot[st] = tcol[...].T[0:8, :]
    for dx, dl in ((2, 1), (2, 0), (1, 1), (3, 1), (1, 0), (3, 0), (0, 1)):
        send(tot.at[st], tot.at[st], 12, totsem.at[0], (tm, sat(dx, dl)))

    def hand_on(q, n, dx, i):
        part = fr.at[q, pl.ds(8 * n, 8)]
        return pltpu.make_async_remote_copy(part, part, ssem.at[i], f3sem.at[2 * q + n], device_id=(tm, sat(dx)), device_id_type=MESH)

    def handed_part(q, n):
        arrive(fr.at[q, pl.ds(8 * n, 8)], f3sem.at[2 * q + n])

    @pl.when(mine)
    def _():
        near = fr.at[quarter, zh * 8 + y * 2 + c]
        pltpu.make_async_copy(near, near, f2sem.at[2]).wait()
        arrive(fr.at[quarter, pl.ds(0, 7)], f2sem.at[zh])
        hand_on(quarter, zh, 1, 16).start()
        hand_on(quarter, zh, 3, 17).start()
        arrive(fr.at[quarter, pl.ds(0, 8)], f2sem.at[1 - zh])
        hand_on(quarter, 1 - zh, 1, 18).start()
        hand_on(quarter, 1 - zh, 3, 19).start()

    arrive(tot.at[pl.ds(0, 7)], totsem.at[0])
    sums = tot[0]
    for b in range(1, 8):
        sums = sums + tot[b]
    tsum[...] = sums
    tcol[...] = jnp.broadcast_to(sums[0:1, :], (128, 256)).T
    norm = tcol[pl.ds(0, rows), :]
    for h in range(2):
        for q in range(2):
            cols = pl.ds(h * half + q * 128, 128)
            w[h, c, tm // 2, :, pl.ds(q * 128, 128)] = (acc[0, :, cols] / norm).astype(BF16)

    def w_send(h, who, dy, dz, dc=0):
        send(w.at[h, c, who // 2], w.at[h, c, who // 2], 14 + h, coresem.at[h] if dc else wsem.at[h, who // 2], (at(dy, dz, dc), st))

    def w_arrive(h, who):
        arrive(w.at[h, c, who // 2], wsem.at[h, who // 2])

    w_send(0, tm, 0, 1)
    for dy in YS:
        w_send(1, tm, dy, 0)
    for dy in YS:
        w_send(0, tm, dy, 0)
    w_send(1, tm, 0, 1)
    w_send(0, tm, 0, 0, 1)
    w_send(1, tm, 0, 0, 1)
    send(tsum, first, 13, firstsem.at[0], (prev, st))

    opp = at(0, 1)
    w_arrive(0, opp)
    for dy in YS:
        w_send(0, opp, dy, 0)
    w_send(0, opp, 0, 0, 1)
    for dy in (1, 3, 2):
        who = at(dy, 0)
        w_arrive(1, who)
        w_send(1, who, 0, 1)
        w_send(1, who, 0, 0, 1)
    for q in range(2):
        away = (x + 4 - 2 * c - q) % 4

        @pl.when(away == 1)
        def _(q=q):
            handed_part(q, zh)
            hand_on(q, zh, 1, 20).start()

        @pl.when(away == 3)
        def _(q=q):
            handed_part(q, 1 - zh)
            hand_on(q, 1 - zh, 3, 20).start()

    for dy in (1, 3, 2):
        who = at(dy, 0)
        w_arrive(0, who)
        w_send(0, who, 0, 0, 1)
    w_arrive(1, opp)
    w_send(1, opp, 0, 0, 1)
    for dy in (1, 3):
        for h in (0, 1):
            who = at(dy, 1)
            w_arrive(h, who)
            w_send(h, who, 0, 0, 1)
    arrive(first, firstsem.at[0])
    lanes = lax.broadcasted_iota(jnp.int32, (8, 256), 1)
    here = pltpu.roll(tsum[...], 255, 1)
    there = jnp.broadcast_to(first[...][:, 0:1], (8, 256))
    loglik[...] = jnp.log(jnp.where(lanes == rows - 1, there, here))
    for h in (0, 1):
        who = at(2, 1)
        w_arrive(h, who)
        w_send(h, who, 0, 0, 1)
    for q in range(2):
        away = (x + 4 - 2 * c - q) % 4
        pl.when(jnp.logical_or(away == 2, away == 3))(functools.partial(handed_part, q, zh))
        pl.when(jnp.logical_or(away == 2, away == 1))(functools.partial(handed_part, q, 1 - zh))
        lies = jnp.concatenate([fr[q, pl.ds(8 * k + 2 * n, 2)].reshape(group, 128) for n in range(4) for k in range(2)], axis=0)
        later = pltpu.roll(lies.astype(F32), 1, 0).reshape(8, 2, rows, 128)
        for k in range(2):
            lt[k, pl.ds(q * 128, 128), :] = later[:, k].reshape(8 * rows, 128).T.astype(BF16)
    at_rows = pl.ds(pl.multiple_of(tm * 256, 256), 256)
    scale = STATES * STATES / time_total
    for h in range(2):
        pair[h] = jnp.dot(lt[c], w[h, c].reshape(8 * rows, half), preferred_element_type=F32)
    for h in range(2):
        arrive(w.at[h, 1 - c], coresem.at[h])
        both = pair[h] + jnp.dot(lt[1 - c], w[h, 1 - c].reshape(8 * rows, half), preferred_element_type=F32)
        at_cols = pl.ds(h * half, half)
        counts[:, at_cols] = am[at_rows, at_cols].astype(F32) * both * scale

    sent(cs, 0)
    sent(fg.at[pl.ds(0, 7), own], 1)
    sent(fg.at[pl.ds(0, 7), head], 2)
    sent(fg.at[0, head], 3)
    for i, ref in enumerate((p1s, p1sc, q1s, q1sc, q2s, q2sc, p2s, p2sc)):
        sent(ref, 4 + i)
    sent(tot.at[pl.ds(0, 7)], 12)
    sent(tsum, 13)
    for h in range(2):
        sent(w.at[h, 0], 14 + h)
        sent(w.at[h, 1, pl.ds(0, 7)], 14 + h)
    for to, cp in handed:
        pl.when(to != tm)(cp.wait_send)

    @pl.when(mine)
    def _():
        for n, (m, dx) in enumerate(((zh, 1), (zh, 3), (1 - zh, 1), (1 - zh, 3))):
            hand_on(quarter, m, dx, 16 + n).wait_send()

    sent(fr.at[0, pl.ds(0, 8)], 20)


def place(counts, loglik, counts_out, loglik_out):
    counts_out[...] = counts[...]
    loglik_out[...] = loglik[0, 0:loglik_out.shape[0]]


def shards(spikes, log_rate, forward, backward, transition, rate_total, edge_weight, block_mask):
    rows = forward.shape[0]
    time_total = spikes.shape[0]
    neurons, width = log_rate.shape
    vm = pltpu.VMEM
    dma = pltpu.SemaphoreType.DMA
    scratch = [
        pltpu.SMEM(block_mask.shape, jnp.int32), vm((2, 256, 8 * rows), BF16), vm((8, 2 * rows, neurons), jnp.int32), vm((neurons, width), BF16), vm((rows, width), BF16), vm((rows, width), F32),
        vm((STATES, width), BF16), vm((STATES, width), BF16), vm((1, width), F32), vm((1, width), F32), vm((2, 256, 256), F32),
        vm((8, 16 + rows, width), BF16), vm((2, 16, rows, 128), BF16),
        vm((8, rows, width), F32), vm((8, rows, width), F32), vm((8, rows, width), F32),
    ]
    for n in (6, 4, 3, 1):
        scratch += [vm((n, rows, 256), I16), vm((n, rows, 256), I16), vm((n, 8, 256), F32), vm((n, 8, 256), F32)]
    scratch += [
        vm((16 + rows, width), F32), vm((256, 128), F32), vm((8, 8, 256), F32), vm((8, 256), F32), vm((8, 256), F32), vm((2, 2, 8, rows, 256), BF16),
        dma((16,)), dma((21,)), dma((8,)), dma((1,)), dma((8,)), dma((1,)), dma((8,)), dma((3,)), dma((4,)),
        dma((2, 6)), dma((2, 4)), dma((2, 3)), dma((2,)), dma((1,)), dma((1,)), dma((2, 8)), dma((2,)),
    ]
    hbm = pl.BlockSpec(memory_space=pl.ANY)
    counts, loglik = pl.pallas_call(
        functools.partial(kernel, time_total),
        out_shape=(vm((256, width), F32), vm((8, 256), F32)),
        in_specs=[hbm] * 8,
        out_specs=(pl.BlockSpec(memory_space=pltpu.VMEM), pl.BlockSpec(memory_space=pltpu.VMEM)),
        scratch_shapes=scratch,
        compiler_params=pltpu.CompilerParams(collective_id=0, has_side_effects=True, vmem_limit_bytes=56 * 2**20),
    )(spikes, log_rate, forward, backward, transition, rate_total.reshape(1, width), edge_weight.reshape(1, width), block_mask)
    return pl.pallas_call(
        place,
        out_shape=(jax.ShapeDtypeStruct((256, width), F32), jax.ShapeDtypeStruct((rows,), F32)),
    )(pltpu.with_memory_space_constraint(counts, pltpu.VMEM), pltpu.with_memory_space_constraint(loglik, pltpu.VMEM))


def solution(mesh):
    in_specs = (P(None, "tm"), P("tm", "state"), P("tm", "state"), P("tm", "state"), P(None, "state"), P("state"), P("state"), P())
    out_specs = (P("tm", "state"), P("tm"))
    return jax.shard_map(shards, mesh=mesh, in_specs=in_specs, out_specs=out_specs, check_vma=False)
```

```python
import functools
import jax
import jax.numpy as jnp
from jax import lax
from jax.experimental import pallas as pl
from jax.experimental.pallas import tpu as pltpu
from jax.sharding import PartitionSpec as P

MESH = pl.DeviceIdType.MESH
STATES = 4096
BLOCK = 128
F32, BF16, I16 = jnp.float32, jnp.bfloat16, jnp.int16
TOP = 32760.0
ROUND = 12582912.0
STEPS = ((2, 1), (1, 1), (3, 1), (0, 1), (2, 0), (1, 0), (3, 0), (0, 0))
YS = (2, 1, 3)
EARLY = 3
RELAY = 3


def encode(value):
    most = jnp.maximum(jnp.max(jnp.abs(value), axis=0, keepdims=True), 1e-30)
    coded = (value * (TOP / most) + ROUND) - ROUND
    unit = most * (1.0 / TOP)
    first = lax.broadcasted_iota(jnp.int32, (8, 128), 0) == 0
    packed = jnp.where(first, jnp.broadcast_to(unit[:, 0:128], (8, 128)), jnp.broadcast_to(unit[:, 128:256], (8, 128)))
    return coded.astype(jnp.int32).astype(I16), packed


def decode(coded, scale):
    unit = jnp.concatenate([scale[0:1, :], scale[1:2, :]], axis=1)
    return coded.astype(jnp.int32).astype(F32) * unit


def kernel(time_total, spikes, log_rate, forward, backward, transition, rate, edge, block_mask,
           counts, loglik,
           mask, lt, spk, lr, fw, bw, tr, am, rt, ew, pair,
           fg, fr, cs, cr, acc,
           p1s, p1r, p1sc, p1rc, q1s, q1r, q1sc, q1rc, q2s, q2r, q2sc, q2rc, p2s, p2r, p2sc, p2rc,
           car, tcol, tot, tsum, first, w,
           lsem, ssem, csem, tailsem, f1sem, f1tsem, handsem, f2sem, f3sem, p1sem, q1sem, q2sem, p2sem, totsem, firstsem, wsem, coresem):
    tm, st = lax.axis_index("tm"), lax.axis_index("state")
    y, zh, c = tm // 4, (tm // 2) % 2, tm % 2
    zl, x = st // 4, st % 4

    def at(dy=0, dz=0, dc=0):
        return (((y + dy) % 4) * 2 + (zh + dz) % 2) * 2 + (c + dc) % 2

    def sat(dx=0, dl=0):
        return ((zl + dl) % 2) * 4 + (x + dx) % 4

    rows = fw.shape[0]
    group = 2 * rows
    half = 256

    def local(src, dst, i):
        cp = pltpu.make_async_copy(src, dst, lsem.at[i])
        cp.start()
        return cp

    def spike_load(s):
        dy, dz = STEPS[s]
        row = pl.multiple_of((((y + dy) % 4) * 2 + (zh + dz) % 2) * group, group)
        return local(spikes.at[pl.ds(row, group), :], spk.at[s % spk.shape[0]], s % spk.shape[0])

    loads = {}
    load_fw = local(forward, fw, 8)
    load_lr = local(log_rate, lr, 9)
    for s in range(spk.shape[0]):
        loads[s] = spike_load(s)
    load_tr = local(transition, tr, 10)
    load_mask = local(block_mask, mask, 15)
    load_bw = local(backward, bw, 11)
    load_rt = local(rate, rt, 12)
    load_ew = local(edge, ew, 13)

    barrier = pltpu.get_barrier_semaphore()
    prev, nxt = (tm + 15) % 16, (tm + 1) % 16
    peers = [(at(dc=1), st)] + [(at(dy, dz, dc), st) for dy in range(4) for dz in range(2) for dc in range(2) if (dy != 0) != (dz != 0)]
    peers += [(tm, sat(dx, dl)) for dx in range(4) for dl in range(2) if (dx, dl) != (0, 0)]
    peers += [(prev, st), (nxt, st)]
    for peer in peers:
        pl.semaphore_signal(barrier, inc=1, device_id=peer, device_id_type=MESH)

    def send(src, dst, i, rsem, device):
        pltpu.make_async_remote_copy(src, dst, ssem.at[i], rsem, device_id=device, device_id_type=MESH).start()

    def sent(ref, i):
        pltpu.make_async_remote_copy(ref, ref, ssem.at[i], ssem.at[i], device_id=(tm, st), device_id_type=MESH).wait_send()

    def arrive(dst, rsem):
        pltpu.make_async_remote_copy(dst, dst, ssem.at[0], rsem, device_id=(tm, st), device_id_type=MESH).wait_recv()


    def drive(s):
        loads[s].wait()
        part = jnp.dot(spk[s % spk.shape[0]].astype(F32).astype(BF16), lr[...], preferred_element_type=F32)
        parts = part.reshape(2, rows, 512)
        acc[s] = jnp.where(c == 0, parts[0], parts[1])
        cs[s] = jnp.where(c == 0, parts[1], parts[0])
        if s + spk.shape[0] < 8:
            loads[s + spk.shape[0]] = spike_load(s + spk.shape[0])

    def swap(s):
        send(cs.at[s], cr.at[s], 0, csem.at[s], (at(dc=1), st))

    def pair_up(s):
        dy, dz = STEPS[s]
        arrive(cr.at[s], csem.at[s])
        if dy != 0:
            i = dz * 3 + dy - 1
            p1s[i], p1sc[i] = encode(acc[s, :, 0:half] + cr[s, :, 0:half])
            to = (at(dy), st)
            send(p1s.at[i], p1r.at[i], 4, p1sem.at[0, i], to)
            send(p1sc.at[i], p1rc.at[i], 5, p1sem.at[1, i], to)
        else:
            acc[s, :, 0:half] += cr[s, :, 0:half]
        if dz != 0:
            q1s[dy], q1sc[dy] = encode(acc[s, :, half:] + cr[s, :, half:])
            to = (at(0, 1), st)
            send(q1s.at[dy], q1r.at[dy], 6, q1sem.at[0, dy], to)
            send(q1sc.at[dy], q1rc.at[dy], 7, q1sem.at[1, dy], to)
        else:
            acc[s, :, half:] += cr[s, :, half:]

    def q_second(s):
        dy, _ = STEPS[s]
        arrive(q1r.at[dy], q1sem.at[0, dy])
        arrive(q1rc.at[dy], q1sem.at[1, dy])
        value = acc[s, :, half:] + decode(q1r[dy], q1rc[dy])
        if dy == 0:
            acc[s, :, half:] = value
        else:
            i = dy - 1
            q2s[i], q2sc[i] = encode(value)
            to = (at(dy), st)
            send(q2s.at[i], q2r.at[i], 8, q2sem.at[0, i], to)
            send(q2sc.at[i], q2rc.at[i], 9, q2sem.at[1, i], to)

    def p_sum(s):
        dz = STEPS[s][1]
        value = acc[s, :, 0:half]
        for dy in YS:
            i = dz * 3 + dy - 1
            arrive(p1r.at[i], p1sem.at[0, i])
            arrive(p1rc.at[i], p1sem.at[1, i])
            value = value + decode(p1r[i], p1rc[i])
        return value

    own = pl.ds(16, rows)
    head = pl.ds(0, 16)

    def spread(who, dx, dl):
        send(fg.at[who, own], fg.at[who, own], 1, f1sem.at[who], (tm, sat(dx, dl)))

    load_fw.wait()
    fg[st, 16:16 + rows, :] = fw[...]
    load_lr.wait()
    drive(0)
    pl.semaphore_wait(barrier, len(peers))
    swap(0)
    send(fg.at[st, pl.ds(rows, 16)], fg.at[st, head], 3, tailsem.at[0], (nxt, st))
    spread(st, 0, 1)
    for dx in (1, 3, 2):
        spread(st, dx, 0)
    other = sat(0, 1)
    for s in range(8):
        if s < 7:
            drive(s + 1)
            swap(s + 1)
        pair_up(s)
        if s == 3:
            arrive(fg.at[st, head], tailsem.at[0])
            for dx in range(4):
                for dl in range(2):
                    if (dx, dl) != (0, 0):
                        send(fg.at[st, head], fg.at[st, head], 2, f1tsem.at[0], (tm, sat(dx, dl)))
        if s == RELAY:
            arrive(fg.at[other, own], f1sem.at[other])
            for dx in (1, 3, 2):
                spread(other, dx, 0)

    value = p_sum(3)
    p2s[0], p2sc[0] = encode(value)
    to = (at(0, 1), st)
    send(p2s.at[0], p2r.at[0], 10, p2sem.at[0], to)
    send(p2sc.at[0], p2rc.at[0], 11, p2sem.at[1], to)

    load_tr.wait()
    load_mask.wait()

    @pl.loop(0, STATES // BLOCK)
    def _(ib):
        for cb in range(4):
            jb = st * 4 + cb
            keep = jnp.maximum(mask[ib, jb], (ib == jb).astype(jnp.int32)).astype(F32)
            at_rows = pl.ds(pl.multiple_of(ib * BLOCK, BLOCK), BLOCK)
            at_cols = pl.ds(cb * BLOCK, BLOCK)
            am[at_rows, at_cols] = (tr[at_rows, at_cols].astype(F32) * keep).astype(BF16)

    q_second(4)
    q_second(5)
    q_second(6)
    q_second(7)

    owner = x // 2
    quarter = x % 2
    mine = c == owner
    qcols = pl.ds(pl.multiple_of(x * 128, 128), 128)
    handed = []
    arrive(fg.at[pl.ds(0, 7), head], f1tsem.at[0])
    for n, (dx, dl) in enumerate(((0, 0), (0, 1), (1, 0), (3, 0), (2, 0), (1, 1), (3, 1), (2, 1))):
        who = sat(dx, dl)
        if n > 1:
            arrive(fg.at[who, own], f1sem.at[who])
        src = fg.at[who, own, qcols]
        dst = fr.at[quarter, zh * 8 + y * 2 + c]
        to = who * 2 + owner
        cp = pltpu.make_async_remote_copy(src, dst, handsem.at[n], f2sem.at[zh], device_id=(to, st), device_id_type=MESH)
        pl.when(to == tm)(pltpu.make_async_copy(src, dst, f2sem.at[2]).start)
        pl.when(to != tm)(cp.start)
        handed.append((to, cp))
        part = jnp.dot(fg[who], am[pl.ds(pl.multiple_of(who * 512, 512), 512), :], preferred_element_type=F32)
        car[...] = part if n == 0 else car[...] + part
    load_bw.wait()
    load_rt.wait()
    load_ew.wait()
    value = p_sum(7)
    arrive(p2r.at[0], p2sem.at[0])
    arrive(p2rc.at[0], p2sem.at[1])
    p_drive = value + decode(p2r[0], p2rc[0])
    q_drive = acc[7, :, half:]
    for dy in YS:
        i = dy - 1
        arrive(q2r.at[i], q2sem.at[0, i])
        arrive(q2rc.at[i], q2sem.at[1, i])
        q_drive = q_drive + decode(q2r[i], q2rc[i])
    moved = pltpu.roll(car[...], 1, 0)
    is_edge = jnp.logical_and(lax.broadcasted_iota(jnp.int32, (rows, half), 0) == 0, tm == 0)
    ahead = []
    total = jnp.zeros((rows, 1), F32)
    for h, drive_sum in enumerate((p_drive, q_drive)):
        cols = slice(h * half, (h + 1) * half)
        term = jnp.exp(drive_sum - rt[:, cols]) * bw[:, cols]
        term = jnp.where(is_edge, jnp.broadcast_to(ew[:, cols], (rows, half)), term)
        acc[0, :, cols] = term
        carried = moved[16:, cols]
        total = total + jnp.sum(term * carried, axis=1, keepdims=True)
    tcol[pl.ds(0, rows), :] = jnp.broadcast_to(total, (rows, 128))
    tcol[pl.ds(rows, 256 - rows), :] = jnp.ones((256 - rows, 128), F32)
    tot[st] = tcol[...].T[0:8, :]
    for dx, dl in ((2, 1), (2, 0), (1, 1), (3, 1), (1, 0), (3, 0), (0, 1)):
        send(tot.at[st], tot.at[st], 12, totsem.at[0], (tm, sat(dx, dl)))

    def hand_on(q, n, dx, i):
        part = fr.at[q, pl.ds(8 * n, 8)]
        return pltpu.make_async_remote_copy(part, part, ssem.at[i], f3sem.at[2 * q + n], device_id=(tm, sat(dx)), device_id_type=MESH)

    def handed_part(q, n):
        arrive(fr.at[q, pl.ds(8 * n, 8)], f3sem.at[2 * q + n])

    @pl.when(mine)
    def _():
        near = fr.at[quarter, zh * 8 + y * 2 + c]
        pltpu.make_async_copy(near, near, f2sem.at[2]).wait()
        arrive(fr.at[quarter, pl.ds(0, 7)], f2sem.at[zh])
        hand_on(quarter, zh, 1, 16).start()
        hand_on(quarter, zh, 3, 17).start()
        arrive(fr.at[quarter, pl.ds(0, 8)], f2sem.at[1 - zh])
        hand_on(quarter, 1 - zh, 1, 18).start()
        hand_on(quarter, 1 - zh, 3, 19).start()

    arrive(tot.at[pl.ds(0, 7)], totsem.at[0])
    sums = tot[0]
    for b in range(1, 8):
        sums = sums + tot[b]
    tsum[...] = sums
    tcol[...] = jnp.broadcast_to(sums[0:1, :], (128, 256)).T
    norm = tcol[pl.ds(0, rows), :]
    for h in range(2):
        for q in range(2):
            cols = pl.ds(h * half + q * 128, 128)
            w[h, c, tm // 2, :, pl.ds(q * 128, 128)] = (acc[0, :, cols] / norm).astype(BF16)

    def w_send(h, who, dy, dz, dc=0):
        send(w.at[h, c, who // 2], w.at[h, c, who // 2], 14 + h, coresem.at[h] if dc else wsem.at[h, who // 2], (at(dy, dz, dc), st))

    def w_arrive(h, who):
        arrive(w.at[h, c, who // 2], wsem.at[h, who // 2])

    w_send(0, tm, 0, 1)
    for dy in YS:
        w_send(1, tm, dy, 0)
    for dy in YS:
        w_send(0, tm, dy, 0)
    w_send(1, tm, 0, 1)
    w_send(0, tm, 0, 0, 1)
    w_send(1, tm, 0, 0, 1)
    send(tsum, first, 13, firstsem.at[0], (prev, st))

    opp = at(0, 1)
    w_arrive(0, opp)
    for dy in YS:
        w_send(0, opp, dy, 0)
    w_send(0, opp, 0, 0, 1)
    for dy in (1, 3, 2):
        who = at(dy, 0)
        w_arrive(1, who)
        w_send(1, who, 0, 1)
        w_send(1, who, 0, 0, 1)
    for q in range(2):
        away = (x + 4 - 2 * c - q) % 4

        @pl.when(away == 1)
        def _(q=q):
            handed_part(q, zh)
            hand_on(q, zh, 1, 20).start()

        @pl.when(away == 3)
        def _(q=q):
            handed_part(q, 1 - zh)
            hand_on(q, 1 - zh, 3, 20).start()

    for dy in (1, 3, 2):
        who = at(dy, 0)
        w_arrive(0, who)
        w_send(0, who, 0, 0, 1)
    w_arrive(1, opp)
    w_send(1, opp, 0, 0, 1)
    for dy in (1, 3):
        for h in (0, 1):
            who = at(dy, 1)
            w_arrive(h, who)
            w_send(h, who, 0, 0, 1)
    arrive(first, firstsem.at[0])
    lanes = lax.broadcasted_iota(jnp.int32, (8, 256), 1)
    here = pltpu.roll(tsum[...], 255, 1)
    there = jnp.broadcast_to(first[...][:, 0:1], (8, 256))
    loglik[...] = jnp.log(jnp.where(lanes == rows - 1, there, here))
    for h in (0, 1):
        who = at(2, 1)
        w_arrive(h, who)
        w_send(h, who, 0, 0, 1)
    for q in range(2):
        away = (x + 4 - 2 * c - q) % 4
        pl.when(jnp.logical_or(away == 2, away == 3))(functools.partial(handed_part, q, zh))
        pl.when(jnp.logical_or(away == 2, away == 1))(functools.partial(handed_part, q, 1 - zh))
        lies = jnp.concatenate([fr[q, pl.ds(8 * k + 2 * n, 2)].reshape(group, 128) for n in range(4) for k in range(2)], axis=0)
        later = pltpu.roll(lies.astype(F32), 1, 0).reshape(8, 2, rows, 128)
        for k in range(2):
            lt[k, pl.ds(q * 128, 128), :] = later[:, k].reshape(8 * rows, 128).T.astype(BF16)
    at_rows = pl.ds(pl.multiple_of(tm * 256, 256), 256)
    scale = STATES * STATES / time_total
    for h in range(2):
        pair[h] = jnp.dot(lt[c], w[h, c].reshape(8 * rows, half), preferred_element_type=F32)
    for h in range(2):
        arrive(w.at[h, 1 - c], coresem.at[h])
        both = pair[h] + jnp.dot(lt[1 - c], w[h, 1 - c].reshape(8 * rows, half), preferred_element_type=F32)
        at_cols = pl.ds(h * half, half)
        counts[:, at_cols] = am[at_rows, at_cols].astype(F32) * both * scale

    sent(cs, 0)
    sent(fg.at[pl.ds(0, 7), own], 1)
    sent(fg.at[pl.ds(0, 7), head], 2)
    sent(fg.at[0, head], 3)
    for i, ref in enumerate((p1s, p1sc, q1s, q1sc, q2s, q2sc, p2s, p2sc)):
        sent(ref, 4 + i)
    sent(tot.at[pl.ds(0, 7)], 12)
    sent(tsum, 13)
    for h in range(2):
        sent(w.at[h, 0], 14 + h)
        sent(w.at[h, 1, pl.ds(0, 7)], 14 + h)
    for to, cp in handed:
        pl.when(to != tm)(cp.wait_send)

    @pl.when(mine)
    def _():
        for n, (m, dx) in enumerate(((zh, 1), (zh, 3), (1 - zh, 1), (1 - zh, 3))):
            hand_on(quarter, m, dx, 16 + n).wait_send()

    sent(fr.at[0, pl.ds(0, 8)], 20)


def place(counts, loglik, counts_out, loglik_out):
    counts_out[...] = counts[...]
    loglik_out[...] = loglik[0, 0:loglik_out.shape[0]]


def shards(spikes, log_rate, forward, backward, transition, rate_total, edge_weight, block_mask):
    rows = forward.shape[0]
    time_total = spikes.shape[0]
    neurons, width = log_rate.shape
    vm = pltpu.VMEM
    dma = pltpu.SemaphoreType.DMA
    scratch = [
        pltpu.SMEM(block_mask.shape, jnp.int32), vm((2, 256, 8 * rows), BF16), vm((8, 2 * rows, neurons), jnp.int32), vm((neurons, width), BF16), vm((rows, width), BF16), vm((rows, width), F32),
        vm((STATES, width), BF16), vm((STATES, width), BF16), vm((1, width), F32), vm((1, width), F32), vm((2, 256, 256), F32),
        vm((8, 16 + rows, width), BF16), vm((2, 16, rows, 128), BF16),
        vm((8, rows, width), F32), vm((8, rows, width), F32), vm((8, rows, width), F32),
    ]
    for n in (6, 4, 3, 1):
        scratch += [vm((n, rows, 256), I16), vm((n, rows, 256), I16), vm((n, 8, 128), F32), vm((n, 8, 128), F32)]
    scratch += [
        vm((16 + rows, width), F32), vm((256, 128), F32), vm((8, 8, 256), F32), vm((8, 256), F32), vm((8, 256), F32), vm((2, 2, 8, rows, 256), BF16),
        dma((16,)), dma((21,)), dma((8,)), dma((1,)), dma((8,)), dma((1,)), dma((8,)), dma((3,)), dma((4,)),
        dma((2, 6)), dma((2, 4)), dma((2, 3)), dma((2,)), dma((1,)), dma((1,)), dma((2, 8)), dma((2,)),
    ]
    hbm = pl.BlockSpec(memory_space=pl.ANY)
    counts, loglik = pl.pallas_call(
        functools.partial(kernel, time_total),
        out_shape=(vm((256, width), F32), vm((8, 256), F32)),
        in_specs=[hbm] * 8,
        out_specs=(pl.BlockSpec(memory_space=pltpu.VMEM), pl.BlockSpec(memory_space=pltpu.VMEM)),
        scratch_shapes=scratch,
        compiler_params=pltpu.CompilerParams(collective_id=0, has_side_effects=True, vmem_limit_bytes=56 * 2**20),
    )(spikes, log_rate, forward, backward, transition, rate_total.reshape(1, width), edge_weight.reshape(1, width), block_mask)
    return pl.pallas_call(
        place,
        out_shape=(jax.ShapeDtypeStruct((256, width), F32), jax.ShapeDtypeStruct((rows,), F32)),
    )(pltpu.with_memory_space_constraint(counts, pltpu.VMEM), pltpu.with_memory_space_constraint(loglik, pltpu.VMEM))


def solution(mesh):
    in_specs = (P(None, "tm"), P("tm", "state"), P("tm", "state"), P("tm", "state"), P(None, "state"), P("state"), P("state"), P())
    out_specs = (P("tm", "state"), P("tm"))
    return jax.shard_map(shards, mesh=mesh, in_specs=in_specs, out_specs=out_specs, check_vma=False)
```
